128 devices in a mesh: leaf: 8 (over x, core), panel: 16 (over z, y).
Axes of the slice: x: 4, y: 4, z: 4, core: 2. Of those that a mesh axis runs over, the one named last changes fastest.
Arguments:
- potentials: float32 [131072, 384], P(('leaf', 'panel')), may hold values from -6 to 6
- leaf_to_panel: int32 [131072], P(('leaf', 'panel')), may hold values from 0 to 131071, as said below
- density: bfloat16 [131072, 384], P(('leaf', 'panel')), may hold values from -6 to 6
- corrections: bfloat16 [4096, 384, 384], P(('leaf', 'panel')), may hold values from -0.3125 to 0.3125
- correction_rows: int32 [4096], P(('leaf', 'panel')), may hold values from 0 to 131071, as said below
- correction_cols: int32 [4096], P(('leaf', 'panel')), may hold values from 0 to 131071, as said below
- block_count: int32 [128], P(('leaf', 'panel')), may hold values from 16 to 32, as said below
Outputs:
- velocity: float32 [131072, 384], P(('leaf', 'panel'))
The draws below stay inside these ranges and needn't reach their ends.
Inputs may be any that keep to these rules, and one draw needn't show every extreme that they name: `leaf_to_panel`: device f holds leaf blocks f * 1024 to (f + 1) * 1024 - 1 and panel blocks likewise; the map is a bijection; at most 16 of one device's leaf blocks map to the panel blocks of any one device; exactly 16 map to its own, and exactly 16 to one other device. `correction_rows`: slot s of device f is entry f * 32 + s; its target lies among the panel blocks of devices f - 1, f and f + 1, cyclically. `correction_cols`: A slot's source block lies within 512 blocks of its target, cyclically, and among the panel blocks of devices f - 1, f and f + 1. `block_count`: some device has all 32 slots live.
All inputs are finite; a program needn't handle non-finite values.
Results may differ from the reference program's by a relative error of at most 0.0003.
Values may be sent and summed in bfloat16 or wider, within the bound.
No kernel may reach another device: no remote copies, remote signals or barrier semaphores. Data moves between devices by JAX's collectives and lax.ppermute only.
A program may use at most 64 MiB of HBM per device.

```python
import jax
import jax.numpy as jnp
from jax import lax

BW = 384
BLK_DEV = 1024
NNZ_CAP = 32
CAP = 16
NBLK = 131072
N_LEAF = 8
N_PANEL = 16
DEVICES = 128


def block_pattern(key):
    k_rows, k_cols = jax.random.split(key)
    devices = N_LEAF * N_PANEL
    half = BLK_DEV // 2
    owner = jnp.arange(devices * NNZ_CAP, dtype=jnp.int32) // NNZ_CAP
    within = jnp.arange(devices * NNZ_CAP, dtype=jnp.int32) % NNZ_CAP
    row_local = jax.random.randint(k_rows, (devices * NNZ_CAP,), -half, BLK_DEV + half)
    row_local = jnp.where(within == 0, -1 - row_local % half, row_local)
    row_local = jnp.where(within == 1, BLK_DEV + row_local % half, row_local)
    offset = jax.random.randint(k_cols, (devices * NNZ_CAP,), -half, half + 1)
    offset = jnp.where(within == 0, -jnp.abs(offset), jnp.where(within == 1, jnp.abs(offset), offset))
    col_local = jnp.clip(row_local + offset, -BLK_DEV, 2 * BLK_DEV - 1)
    total = devices * BLK_DEV
    targets = (owner * BLK_DEV + row_local) % total
    sources = (owner * BLK_DEV + col_local) % total
    return (targets.astype(jnp.int32), sources.astype(jnp.int32))


def draw_correction_rows(key, part):
    return block_pattern(key)[0]


def draw_correction_cols(key, part):
    return block_pattern(key)[1]


def draw_leaf_to_panel(key, part):
    key = jax.random.fold_in(key, 7)
    k_order, k_offsets, k_shuffle, k_slot, k_special = jax.random.split(key, 5)
    devices = N_LEAF * N_PANEL
    order = jax.random.permutation(k_order, devices).astype(jnp.int32)
    inverse = jnp.zeros((devices,), jnp.int32).at[order].set(jnp.arange(devices, dtype=jnp.int32))
    special = jax.random.randint(k_special, (), 1, devices).astype(jnp.int32)
    pieces = [jnp.zeros((CAP,), jnp.int32), jnp.zeros((CAP,), jnp.int32) + special]
    for step in range(CAP):
        others = jax.random.permutation(jax.random.fold_in(k_offsets, step), devices - 2).astype(jnp.int32)
        pieces.append(1 + (special + others) % (devices - 1))
    offsets = jnp.concatenate(pieces)[:BLK_DEV]
    offsets = offsets[jax.random.permutation(k_shuffle, BLK_DEV)]
    slot_order = jax.random.permutation(k_slot, BLK_DEV).astype(jnp.int32)
    source = jnp.arange(devices, dtype=jnp.int32)[:, None]
    destination = inverse[(order[source] + offsets[None, :]) % devices]
    return (destination * BLK_DEV + slot_order[None, :]).reshape(devices * BLK_DEV).astype(jnp.int32)


def draw_block_count(key, part):
    key = jax.random.fold_in(key, 5)
    k_counts, k_full = jax.random.split(key)
    devices = N_LEAF * N_PANEL
    counts = jax.random.randint(k_counts, (devices,), NNZ_CAP // 2, NNZ_CAP + 1)
    fullest = jax.random.randint(k_full, (), 0, devices)
    return counts.at[fullest].set(NNZ_CAP).astype(jnp.int32)


def steps_of(rng, shape, cuts, smallest, top_value):
    level = 1.0
    for axis_at, parts in cuts:
        heights = jax.random.uniform(jax.random.fold_in(jax.random.fold_in(rng, 6), axis_at), (parts,), jnp.float32, smallest / len(cuts), top_value / len(cuts))
        level = level * jnp.repeat(jnp.exp(heights), shape[axis_at] // parts).reshape((-1,) + (1,) * (len(shape) - 1 - axis_at))
    return level


def noise(key, extent, spread, reach, cuts=(), kind=jnp.bfloat16):
    loudness = steps_of(key, extent, cuts, -0.22, 0.18) if cuts else 1.0
    array = jax.random.normal(key, extent, jnp.float32) * spread * loudness
    return jnp.minimum(jnp.maximum(array, -reach), reach).astype(kind)


def setup_inputs(seed: int = 0) -> dict:
    keys = jax.random.split(jax.random.key(seed), 8)
    potentials = noise(keys[0], (NBLK, BW), 1.0, 6.0, ((0, 128),), jnp.float32)
    leaf_to_panel = draw_leaf_to_panel(jax.random.fold_in(keys[7], 71), 0)
    density = noise(keys[2], (NBLK, BW), 1.0, 6.0, ((0, 128),))
    corrections = noise(keys[3], (DEVICES * NNZ_CAP, BW, BW), BW ** -0.5, 0.3125, ((0, 128),))
    correction_rows = draw_correction_rows(jax.random.fold_in(keys[7], 71), 0)
    correction_cols = draw_correction_cols(jax.random.fold_in(keys[7], 71), 0)
    block_count = draw_block_count(jax.random.fold_in(keys[7], 71), 0)
    return dict(potentials=potentials, leaf_to_panel=leaf_to_panel, density=density, corrections=corrections, correction_rows=correction_rows, correction_cols=correction_cols, block_count=block_count)


def reference(potentials, leaf_to_panel, density, corrections, correction_rows, correction_cols, block_count):
    devices = N_LEAF * N_PANEL
    far_field = jnp.zeros((NBLK, BW), jnp.float32).at[leaf_to_panel].set(potentials.astype(jnp.float32))
    stacked = corrections.reshape(devices, NNZ_CAP, BW, BW)
    sources = correction_cols.reshape(devices, NNZ_CAP)

    def one_owner(pair):
        matrices, columns = pair
        vectors = density[columns].astype(jnp.float32)
        return jnp.einsum("kij,kj->ki", matrices.astype(jnp.float32), vectors)

    terms = lax.map(one_owner, (stacked, sources))
    live = jnp.arange(NNZ_CAP, dtype=jnp.int32)[None, :] < block_count[:, None]
    terms = jnp.where(live[:, :, None], terms, jnp.zeros_like(terms))
    near_field = jnp.zeros((NBLK, BW), jnp.float32).at[correction_rows].add(terms.reshape(devices * NNZ_CAP, BW))
    return far_field + near_field
```

```python
import functools

import jax
import jax.numpy as jnp
from jax import lax
from jax.experimental import pallas as pl
from jax.experimental.pallas import tpu as pltpu
from jax.sharding import PartitionSpec as P

AXES = ("leaf", "panel")
DEV = 128
CAP = 16
ROWS = 1024
BW = 384
TILES = BW // 128
LINES = CAP // 2 * TILES + 1
SLOTS = 32
TOTAL = DEV * ROWS
F32, BF16, I32 = jnp.float32, jnp.bfloat16, jnp.int32
NT = (((1,), (1,)), ((), ()))
VMEM = pl.BlockSpec(memory_space=pltpu.VMEM)
SMEM = pl.BlockSpec(memory_space=pltpu.SMEM)


def iota(shape, dim):
    return lax.broadcasted_iota(I32, shape, dim)


def one_hot(mask):
    return jnp.where(mask, 1.0, 0.0).astype(BF16)


def row16(row):
    return jnp.broadcast_to(row, (16, 128)).astype(BF16)[None]


def times_row(block, row):
    return (block.reshape(8, 16, 128) * row16(row)).reshape(128, 128)


def mm(a, b):
    return jnp.dot(a, b, preferred_element_type=F32)


def pack_kernel(map_ref, pot_ref, out_ref, sel, dig, head):
    for g in range(8):
        rows = pl.ds(g * 128, 128)
        x = pot_ref[rows, :]
        top = jnp.max(jnp.abs(x), axis=1, keepdims=True)
        step = jnp.maximum(top * (1.0 / 32766.0), 2.0**-100)
        expo = jnp.floor(jnp.log2(step) + 1e-3)
        power = jnp.exp2(expo).astype(BF16).astype(F32)
        mant = jnp.maximum(jnp.ceil((step / power - 1.0) * 64.0), 0.0)
        scale = power * (1.0 + mant * (1.0 / 64.0))
        q = jnp.clip(jnp.round(x * (1.0 / scale)), -32767.0, 32767.0)
        hi = jnp.floor(q * (1.0 / 256.0))
        lo = q - hi * 256.0
        for n in range(TILES):
            dig[rows, pl.ds(n * 256, 128)] = hi[:, n * 128 : n * 128 + 128].astype(BF16)
            dig[rows, pl.ds(n * 256 + 128, 128)] = lo[:, n * 128 : n * 128 + 128].astype(BF16)
        lane = iota((128, 128), 1)
        head[rows, :] = jnp.where(lane == 0, expo + 128.0, jnp.where(lane == 1, mant, 0.0)).astype(BF16)
    eye = one_hot(iota((16, 128), 0) == iota((16, 128), 1))
    codes = lax.dot_general(eye, head[...], NT, preferred_element_type=F32)

    place = map_ref[...]
    dest, label = place >> 10, (place & (ROWS - 1)) + 1
    sub = iota((128, 128), 0)
    before = jnp.concatenate([one_hot(sub < iota((128, 128), 1)), one_hot(sub >= 0)], axis=1)
    hits = [dest[b : b + 1, :] == sub for b in range(8)]
    hot = [one_hot(h) for h in hits]
    counts = mm(jnp.concatenate(hot, axis=0), before)
    carry = jnp.zeros((128, 128), F32)
    ranks = []
    for b in range(8):
        part = counts[b * 128 : b * 128 + 128]
        ranks.append(jnp.sum(jnp.where(hits[b], part[:, :128] + carry, 0.0), axis=0, keepdims=True))
        carry = carry + part[:, 128:]

    low = iota((128, 128), 0) & (CAP - 1)
    digits = [[], [], [], []]
    ranked = []
    for b in range(8):
        lanes = pl.ds(b * 128, 128)
        for c in range(CAP):
            at = (c % 8) * 256 + (c // 8) * 128
            sel[pl.ds(at, 128), lanes] = times_row(hot[b], jnp.where(ranks[b] == c, 1.0, 0.0))
        lab = label[b : b + 1, :]
        cols = slice(b * 128, b * 128 + 128)
        for k, row in enumerate(
            ((lab >> 7).astype(F32), (lab & 127).astype(F32), codes[0:1, cols], codes[1:2, cols])
        ):
            digits[k].append(times_row(hot[b], row))
        ranked.append(one_hot(ranks[b].astype(I32) == low))
    left = jnp.concatenate([jnp.concatenate(d, axis=1) for d in digits], axis=0)
    meta = lax.dot_general(left, jnp.concatenate(ranked, axis=1), NT, preferred_element_type=F32).astype(I32)
    words = jnp.where(
        iota((128, 128), 1) < CAP, meta[0:128] * 128 + meta[128:256], meta[256:384] * 128 + meta[384:512]
    )
    out_ref[pl.ds(LINES - 1, DEV, stride=LINES), :] = words

    for n in range(TILES):
        for r in range(8):
            both = mm(sel[pl.ds(r * 256, 256), :], dig[:, pl.ds(n * 256, 256)])
            q = (both[:, :128] * 256.0 + both[:, 128:]).astype(I32)
            out_ref[pl.ds(n * 8 + r, DEV, stride=LINES), :] = (q[128:] << 16) | (q[:128] & 0xFFFF)


def pack(leaf_to_panel, potentials):
    return pl.pallas_call(
        pack_kernel,
        out_shape=jax.ShapeDtypeStruct((DEV * LINES, 128), I32),
        in_specs=[VMEM, VMEM],
        out_specs=VMEM,
        scratch_shapes=[
            pltpu.VMEM((DEV * CAP, ROWS), BF16),
            pltpu.VMEM((ROWS, 2 * BW), BF16),
            pltpu.VMEM((ROWS, 128), BF16),
        ],
        compiler_params=pltpu.CompilerParams(vmem_limit_bytes=40 * 2**20),
        cost_estimate=pl.CostEstimate(flops=2 * DEV * CAP * ROWS * 2 * BW, bytes_accessed=4 * 2**20, transcendentals=0),
        name="pack_rows",
    )(leaf_to_panel.reshape(8, 128), potentials)


def place_kernel(me_ref, msg_ref, own_ref, prev_ref, next_ref, asks_ref, ask_prev_ref, ask_next_ref, out_ref, sel, dig):
    heads = jnp.transpose(msg_ref[pl.ds(LINES - 1, DEV, stride=LINES), :].astype(F32)).astype(I32)
    target = heads[0:CAP] - 1
    code = heads[CAP : 2 * CAP]
    high, low = target >> 7, target & 127
    scale = jnp.exp2((code >> 7).astype(F32) - 128.0).astype(BF16).astype(F32)
    scale = scale * (1.0 + (code & 127).astype(F32) * (1.0 / 64.0))
    sub = iota((128, 128), 0)
    for c in range(CAP):
        hot = one_hot(low[c : c + 1] == sub)
        for g in range(8):
            row = jnp.where(high[c : c + 1] == g, scale[c : c + 1], 0.0)
            sel[pl.ds(g * 128, 128), pl.ds(c * 128, 128)] = times_row(hot, row)
    lane = iota((1, 128), 1)
    base = me_ref[0] * ROWS
    rows = jnp.where(
        lane < SLOTS,
        asks_ref[SLOTS : SLOTS + 1, :],
        jnp.where(lane < 2 * SLOTS, ask_prev_ref[SLOTS : SLOTS + 1, :], ask_next_ref[SLOTS : SLOTS + 1, :]),
    )
    target = jnp.where((rows < 0) | (lane >= 3 * SLOTS), -1, (rows - base) & (TOTAL - 1))
    for g in range(8):
        hot = one_hot(target - g * 128 == sub)
        sel[pl.ds(g * 128, 128), pl.ds(CAP * 128, 128)] = hot
        sel[pl.ds(g * 128, 128), pl.ds(CAP * 128 + 128, 128)] = hot
    near = jnp.concatenate([own_ref[...], prev_ref[...], next_ref[...], jnp.zeros((SLOTS, BW), F32)], axis=0)
    first = near.astype(BF16)
    second = (near - first.astype(F32)).astype(BF16)
    blank = jnp.zeros((256, 128), BF16)
    for n in range(TILES):
        for r in range(8):
            w = msg_ref[pl.ds(n * 8 + r, DEV, stride=LINES), :]
            for c, hi, lo in ((r, (w << 16) >> 24, w & 255), (r + 8, w >> 24, (w >> 16) & 255)):
                dig[pl.ds(c * 128, 128), pl.ds(n * 256, 128)] = hi.astype(F32).astype(BF16)
                dig[pl.ds(c * 128, 128), pl.ds(n * 256 + 128, 128)] = lo.astype(F32).astype(BF16)
        dig[pl.ds(CAP * 128, 256), pl.ds(n * 256, 128)] = blank
        dig[pl.ds(CAP * 128, 128), pl.ds(n * 256 + 128, 128)] = first[:, n * 128 : n * 128 + 128]
        dig[pl.ds(CAP * 128 + 128, 128), pl.ds(n * 256 + 128, 128)] = second[:, n * 128 : n * 128 + 128]
        for g in range(4):
            both = mm(sel[pl.ds(g * 256, 256), :], dig[:, pl.ds(n * 256, 256)])
            out_ref[pl.ds(g * 256, 256), pl.ds(n * 128, 128)] = both[:, :128] * 256.0 + both[:, 128:]


def place(me, arrived, terms, asks):
    return pl.pallas_call(
        place_kernel,
        out_shape=jax.ShapeDtypeStruct((ROWS, BW), F32),
        in_specs=[SMEM] + [VMEM] * 7,
        out_specs=VMEM,
        scratch_shapes=[
            pltpu.VMEM((ROWS, CAP * 128 + 256), BF16),
            pltpu.VMEM((CAP * 128 + 256, 2 * BW), BF16),
        ],
        compiler_params=pltpu.CompilerParams(vmem_limit_bytes=40 * 2**20),
        cost_estimate=pl.CostEstimate(flops=2 * DEV * CAP * ROWS * 2 * BW, bytes_accessed=4 * 2**20, transcendentals=0),
        name="place_rows",
    )(me, arrived, *terms, *asks)


def fetch_kernel(me_ref, asks_ref, ask_prev_ref, ask_next_ref, density_ref, own_ref, prev_ref, next_ref):
    base = me_ref[0] * ROWS
    asked = jnp.concatenate([asks_ref[0:SLOTS, :], ask_prev_ref[0:SLOTS, :], ask_next_ref[0:SLOTS, :]], axis=0)
    at = (asked - base) & (TOTAL - 1)
    lane = iota((3 * SLOTS, 128), 1)
    hot = jnp.concatenate([one_hot(at - b * 128 == lane) for b in range(8)], axis=1)
    got = mm(hot, density_ref[...]).astype(BF16)
    own_ref[...] = got[0:SLOTS]
    prev_ref[...] = got[SLOTS : 2 * SLOTS]
    next_ref[...] = got[2 * SLOTS :]


def fetch(me, asks, density):
    rows = jax.ShapeDtypeStruct((SLOTS, BW), BF16)
    return pl.pallas_call(
        fetch_kernel,
        out_shape=(rows, rows, rows),
        in_specs=[SMEM] + [VMEM] * 4,
        out_specs=(VMEM, VMEM, VMEM),
        cost_estimate=pl.CostEstimate(flops=10**8, bytes_accessed=2**20, transcendentals=0),
        name="fetch_density",
    )(me, *asks, density)


STEP = 4


def term_kernel(count_ref, mats_ref, own_ref, prev_ref, next_ref, out_ref, acc):
    step = pl.program_id(0)

    @pl.when(step == 0)
    def _():
        acc[...] = jnp.zeros_like(acc)

    rows = (own_ref[...].astype(F32) + prev_ref[...].astype(F32) + next_ref[...].astype(F32)).astype(BF16)
    vecs = jnp.concatenate([rows, jnp.zeros((128 - SLOTS, BW), BF16)], axis=0)
    lane = iota((BW, 128), 1)
    total = acc[...]
    for k in range(STEP):
        prod = lax.dot_general(mats_ref[k], vecs, NT, preferred_element_type=F32)
        total = jnp.where(lane == step * STEP + k, prod, total)
    acc[...] = total

    @pl.when(step == SLOTS // STEP - 1)
    def _():
        live = iota((SLOTS, BW), 0) < count_ref[0]
        out_ref[...] = jnp.where(live, jnp.transpose(acc[...])[0:SLOTS], 0.0)


def make_terms(count, mats, rows):
    whole = pl.BlockSpec((SLOTS, BW), lambda i: (0, 0))
    return pl.pallas_call(
        term_kernel,
        grid=(SLOTS // STEP,),
        out_shape=jax.ShapeDtypeStruct((SLOTS, BW), F32),
        in_specs=[SMEM, pl.BlockSpec((STEP, BW, BW), lambda i: (i, 0, 0)), whole, whole, whole],
        out_specs=whole,
        scratch_shapes=[pltpu.VMEM((BW, 128), F32)],
        compiler_params=pltpu.CompilerParams(vmem_limit_bytes=20 * 2**20),
        cost_estimate=pl.CostEstimate(flops=2 * SLOTS * BW * BW * 128, bytes_accessed=SLOTS * BW * BW * 2, transcendentals=0),
        name="near_terms",
    )(count, mats, *rows)


def shift(value, steps):
    return lax.ppermute(value, AXES, [(i, (i + steps) % DEV) for i in range(DEV)])


def on_device(potentials, leaf_to_panel, density, corrections, correction_rows, correction_cols, block_count):
    me = lax.axis_index(AXES).astype(I32).reshape(1)
    live = jnp.arange(SLOTS) < block_count[0]
    ask = jnp.concatenate(
        [
            jnp.broadcast_to(correction_cols[:, None], (SLOTS, 128)),
            jnp.broadcast_to(jnp.tile(jnp.where(live, correction_rows, -1), 4)[None], (8, 128)),
        ],
        axis=0,
    )
    asks = (ask, shift(ask, 1), shift(ask, -1))
    message = pack(leaf_to_panel, potentials)
    arrived = lax.all_to_all(
        message.reshape(DEV, LINES, 1, 128), AXES, split_axis=0, concat_axis=0, tiled=True
    ).reshape(DEV * LINES, 128)
    own, for_prev, for_next = fetch(me, asks, density)
    rows = (own, shift(for_next, 1), shift(for_prev, -1))
    term = make_terms(block_count, corrections, rows)
    terms = (term, shift(term, 1), shift(term, -1))
    return place(me, arrived, terms, asks)


def solution(mesh):
    rows = P(AXES, None)
    flat = P(AXES)
    return jax.shard_map(
        on_device,
        mesh=mesh,
        in_specs=(rows, flat, rows, P(AXES, None, None), flat, flat, flat),
        out_specs=rows,
        check_vma=False,
    )
```

```python
import functools

import jax
import jax.numpy as jnp
from jax import lax
from jax.experimental import pallas as pl
from jax.experimental.pallas import tpu as pltpu
from jax.sharding import PartitionSpec as P

AXES = ("leaf", "panel")
DEV = 128
CAP = 16
ROWS = 1024
BW = 384
TILES = BW // 128
LINES = CAP // 2 * TILES + 1
SLOTS = 32
TOTAL = DEV * ROWS
F32, BF16, I32 = jnp.float32, jnp.bfloat16, jnp.int32
NT = (((1,), (1,)), ((), ()))
VMEM = pl.BlockSpec(memory_space=pltpu.VMEM)
SMEM = pl.BlockSpec(memory_space=pltpu.SMEM)
HBM = pl.BlockSpec(memory_space=pltpu.HBM)


def iota(shape, dim):
    return lax.broadcasted_iota(I32, shape, dim)


def one_hot(mask):
    return jnp.where(mask, 1.0, 0.0).astype(BF16)


def row16(row):
    return jnp.broadcast_to(row, (16, 128)).astype(BF16)[None]


def times_row(block, row):
    return (block.reshape(8, 16, 128) * row16(row)).reshape(128, 128)


def mm(a, b):
    return jnp.dot(a, b, preferred_element_type=F32)


def pack_kernel(map_hbm, pot_hbm, out_hbm, place, pot, msg, sel, dig, head, sems):
    get_map = pltpu.make_async_copy(map_hbm, place, sems.at[0])
    get_map.start()
    get_pot = []
    for g in range(4):
        rows = pl.ds(g * 256, 256)
        get_pot.append(pltpu.make_async_copy(pot_hbm.at[rows], pot.at[rows], sems.at[1 + g]))
        get_pot[g].start()
    get_map.wait()

    dest, label = place[...] >> 10, (place[...] & (ROWS - 1)) + 1
    sub = iota((128, 128), 0)
    before = jnp.concatenate([one_hot(sub < iota((128, 128), 1)), one_hot(sub >= 0)], axis=1)
    hits = [dest[b : b + 1, :] == sub for b in range(8)]
    hot = [one_hot(h) for h in hits]
    counts = mm(jnp.concatenate(hot, axis=0), before)
    carry = jnp.zeros((128, 128), F32)
    ranks = []
    for b in range(8):
        part = counts[b * 128 : b * 128 + 128]
        ranks.append(jnp.sum(jnp.where(hits[b], part[:, :128] + carry, 0.0), axis=0, keepdims=True))
        carry = carry + part[:, 128:]
    low = sub & (CAP - 1)
    ranked = []
    for b in range(8):
        lanes = pl.ds(b * 128, 128)
        for c in range(CAP):
            block = times_row(hot[b], jnp.where(ranks[b] == c, 1.0, 0.0))
            for g in range(8):
                sel[pl.ds(g * 256 + c * 16, 16), lanes] = block[g * 16 : g * 16 + 16]
        ranked.append(one_hot(ranks[b].astype(I32) == low))

    for g in range(8):
        if g % 2 == 0:
            get_pot[g // 2].wait()
        rows = pl.ds(g * 128, 128)
        x = pot[rows, :]
        top = jnp.max(jnp.abs(x), axis=1, keepdims=True)
        step = jnp.maximum(top * (1.0 / 32766.0), 2.0**-100)
        expo = jnp.floor(jnp.log2(step) + 1e-3)
        power = jnp.exp2(expo).astype(BF16).astype(F32)
        mant = jnp.maximum(jnp.ceil((step / power - 1.0) * 64.0), 0.0)
        scale = power * (1.0 + mant * (1.0 / 64.0))
        q = jnp.clip(jnp.round(x * (1.0 / scale)), -32767.0, 32767.0)
        hi = jnp.floor(q * (1.0 / 256.0))
        lo = q - hi * 256.0
        for n in range(TILES):
            dig[rows, pl.ds(n * 256, 128)] = hi[:, n * 128 : n * 128 + 128].astype(BF16)
            dig[rows, pl.ds(n * 256 + 128, 128)] = lo[:, n * 128 : n * 128 + 128].astype(BF16)
        lane = iota((128, 128), 1)
        head[rows, :] = jnp.where(lane == 0, expo + 128.0, jnp.where(lane == 1, mant, 0.0)).astype(BF16)
    eye = one_hot(iota((16, 128), 0) == iota((16, 128), 1))
    codes = lax.dot_general(eye, head[...], NT, preferred_element_type=F32)

    digits = [[], [], [], []]
    for b in range(8):
        lab = label[b : b + 1, :]
        cols = slice(b * 128, b * 128 + 128)
        for k, row in enumerate(
            ((lab >> 7).astype(F32), (lab & 127).astype(F32), codes[0:1, cols], codes[1:2, cols])
        ):
            digits[k].append(times_row(hot[b], row))
    left = jnp.concatenate([jnp.concatenate(d, axis=1) for d in digits], axis=0)
    meta = lax.dot_general(left, jnp.concatenate(ranked, axis=1), NT, preferred_element_type=F32).astype(I32)
    words = jnp.where(
        iota((128, 128), 1) < CAP, meta[0:128] * 128 + meta[128:256], meta[256:384] * 128 + meta[384:512]
    )
    msg[pl.ds(LINES - 1, DEV, stride=LINES), :] = words

    put = []
    for g in range(8):
        for n in range(TILES):
            both = mm(sel[pl.ds(g * 256, 256), :], dig[:, pl.ds(n * 256, 256)])
            q = (both[:, :128] * 256.0 + both[:, 128:]).astype(I32)
            w = (q[128:] << 16) | (q[:128] & 0xFFFF)
            for r in range(8):
                msg[pl.ds(g * 16 * LINES + n * 8 + r, 16, stride=LINES), :] = w[r * 16 : r * 16 + 16]
        lines = pl.ds(g * 16 * LINES, 16 * LINES)
        put.append(pltpu.make_async_copy(msg.at[lines], out_hbm.at[lines], sems.at[5 + g]))
        put[g].start()
    for copy in put:
        copy.wait()


def pack(leaf_to_panel, potentials):
    return pl.pallas_call(
        pack_kernel,
        out_shape=jax.ShapeDtypeStruct((DEV * LINES, 128), I32),
        in_specs=[HBM, HBM],
        out_specs=HBM,
        scratch_shapes=[
            pltpu.VMEM((8, 128), I32),
            pltpu.VMEM((ROWS, BW), F32),
            pltpu.VMEM((DEV * LINES, 128), I32),
            pltpu.VMEM((DEV * CAP, ROWS), BF16),
            pltpu.VMEM((ROWS, 2 * BW), BF16),
            pltpu.VMEM((ROWS, 128), BF16),
            pltpu.SemaphoreType.DMA((13,)),
        ],
        compiler_params=pltpu.CompilerParams(vmem_limit_bytes=60 * 2**20),
        cost_estimate=pl.CostEstimate(flops=2 * DEV * CAP * ROWS * 2 * BW, bytes_accessed=4 * 2**20, transcendentals=0),
        name="pack_rows",
    )(leaf_to_panel.reshape(8, 128), potentials)


def by_slot(lane, own_ref, prev_ref, next_ref, line):
    own, prev, following = (ref[line : line + 1, :] for ref in (own_ref, prev_ref, next_ref))
    return jnp.where(lane < SLOTS, own, jnp.where(lane < 2 * SLOTS, prev, following))


def place_kernel(me_ref, msg_ref, own_ref, prev_ref, next_ref, asks_ref, ask_prev_ref, ask_next_ref, out_ref, sel, dig):
    heads = jnp.transpose(msg_ref[pl.ds(LINES - 1, DEV, stride=LINES), :].astype(F32)).astype(I32)
    target = heads[0:CAP] - 1
    code = heads[CAP : 2 * CAP]
    high, low = target >> 7, target & 127
    scale = jnp.exp2((code >> 7).astype(F32) - 128.0).astype(BF16).astype(F32)
    scale = scale * (1.0 + (code & 127).astype(F32) * (1.0 / 64.0))
    sub = iota((128, 128), 0)
    for c in range(CAP):
        hot = one_hot(low[c : c + 1] == sub)
        for g in range(8):
            row = jnp.where(high[c : c + 1] == g, scale[c : c + 1], 0.0)
            sel[pl.ds(g * 128, 128), pl.ds(c * 128, 128)] = times_row(hot, row)
    lane = iota((1, 128), 1)
    base = me_ref[0] * ROWS
    rows = by_slot(lane, asks_ref, ask_prev_ref, ask_next_ref, 1)
    target = jnp.where((rows < 0) | (lane >= 3 * SLOTS), -1, (rows - base) & (TOTAL - 1))
    for g in range(8):
        hot = one_hot(target - g * 128 == sub)
        sel[pl.ds(g * 128, 128), pl.ds(CAP * 128, 128)] = hot
        sel[pl.ds(g * 128, 128), pl.ds(CAP * 128 + 128, 128)] = hot
    near = jnp.concatenate([own_ref[...], prev_ref[...], next_ref[...], jnp.zeros((SLOTS, BW), F32)], axis=0)
    first = near.astype(BF16)
    second = (near - first.astype(F32)).astype(BF16)
    blank = jnp.zeros((256, 128), BF16)
    for n in range(TILES):
        for r in range(8):
            w = msg_ref[pl.ds(n * 8 + r, DEV, stride=LINES), :]
            for c, hi, lo in ((r, (w << 16) >> 24, w & 255), (r + 8, w >> 24, (w >> 16) & 255)):
                dig[pl.ds(c * 128, 128), pl.ds(n * 256, 128)] = hi.astype(F32).astype(BF16)
                dig[pl.ds(c * 128, 128), pl.ds(n * 256 + 128, 128)] = lo.astype(F32).astype(BF16)
        dig[pl.ds(CAP * 128, 256), pl.ds(n * 256, 128)] = blank
        dig[pl.ds(CAP * 128, 128), pl.ds(n * 256 + 128, 128)] = first[:, n * 128 : n * 128 + 128]
        dig[pl.ds(CAP * 128 + 128, 128), pl.ds(n * 256 + 128, 128)] = second[:, n * 128 : n * 128 + 128]
        for g in range(4):
            both = mm(sel[pl.ds(g * 256, 256), :], dig[:, pl.ds(n * 256, 256)])
            out_ref[pl.ds(g * 256, 256), pl.ds(n * 128, 128)] = both[:, :128] * 256.0 + both[:, 128:]


def place(me, arrived, terms, asks):
    return pl.pallas_call(
        place_kernel,
        out_shape=jax.ShapeDtypeStruct((ROWS, BW), F32),
        in_specs=[SMEM] + [VMEM] * 7,
        out_specs=VMEM,
        scratch_shapes=[
            pltpu.VMEM((ROWS, CAP * 128 + 256), BF16),
            pltpu.VMEM((CAP * 128 + 256, 2 * BW), BF16),
        ],
        compiler_params=pltpu.CompilerParams(vmem_limit_bytes=40 * 2**20),
        cost_estimate=pl.CostEstimate(flops=2 * DEV * CAP * ROWS * 2 * BW, bytes_accessed=4 * 2**20, transcendentals=0),
        name="place_rows",
    )(me, arrived, *terms, *asks)


def fetch_kernel(me_ref, asks_ref, ask_prev_ref, ask_next_ref, density_ref, msg_ref, own_ref, prev_ref, next_ref, out_ref):
    base = me_ref[0] * ROWS
    cols = by_slot(iota((1, 128), 1), asks_ref, ask_prev_ref, ask_next_ref, 0)
    at = ((cols - base) & (TOTAL - 1)).astype(F32)
    at = jnp.transpose(jnp.broadcast_to(at, (128, 128)))[0 : 3 * SLOTS].astype(I32)
    lane = iota((3 * SLOTS, 128), 1)
    hot = jnp.concatenate([one_hot(at - b * 128 == lane) for b in range(8)], axis=1)
    got = mm(hot, density_ref[...]).astype(BF16)
    own_ref[...] = got[0:SLOTS]
    prev_ref[...] = got[SLOTS : 2 * SLOTS]
    next_ref[...] = got[2 * SLOTS :]


def fetch(me, asks, density, message):
    rows = jax.ShapeDtypeStruct((SLOTS, BW), BF16)
    return pl.pallas_call(
        fetch_kernel,
        out_shape=(rows, rows, rows, jax.ShapeDtypeStruct(message.shape, message.dtype)),
        in_specs=[SMEM] + [VMEM] * 4 + [HBM],
        out_specs=(VMEM, VMEM, VMEM, HBM),
        input_output_aliases={5: 3},
        compiler_params=pltpu.CompilerParams(vmem_limit_bytes=105 * 2**19),
        cost_estimate=pl.CostEstimate(flops=10**8, bytes_accessed=2**20, transcendentals=0),
        name="fetch_density",
    )(me, *asks, density, message)


STEP = 4


def term_kernel(count_ref, mats_ref, own_ref, prev_ref, next_ref, out_ref, acc):
    step = pl.program_id(0)

    @pl.when(step == 0)
    def _():
        acc[...] = jnp.zeros_like(acc)

    rows = (own_ref[...].astype(F32) + prev_ref[...].astype(F32) + next_ref[...].astype(F32)).astype(BF16)
    vecs = jnp.concatenate([rows, jnp.zeros((128 - SLOTS, BW), BF16)], axis=0)
    lane = iota((BW, 128), 1)
    total = acc[...]
    for k in range(STEP):
        prod = lax.dot_general(mats_ref[k], vecs, NT, preferred_element_type=F32)
        total = jnp.where(lane == step * STEP + k, prod, total)
    acc[...] = total

    @pl.when(step == SLOTS // STEP - 1)
    def _():
        live = iota((SLOTS, BW), 0) < count_ref[0]
        out_ref[...] = jnp.where(live, jnp.transpose(acc[...])[0:SLOTS], 0.0)


def make_terms(count, mats, rows):
    whole = pl.BlockSpec((SLOTS, BW), lambda i: (0, 0))
    return pl.pallas_call(
        term_kernel,
        grid=(SLOTS // STEP,),
        out_shape=jax.ShapeDtypeStruct((SLOTS, BW), F32),
        in_specs=[SMEM, pl.BlockSpec((STEP, BW, BW), lambda i: (i, 0, 0)), whole, whole, whole],
        out_specs=whole,
        scratch_shapes=[pltpu.VMEM((BW, 128), F32)],
        compiler_params=pltpu.CompilerParams(vmem_limit_bytes=20 * 2**20),
        cost_estimate=pl.CostEstimate(flops=6 * 10**10, bytes_accessed=SLOTS * BW * BW * 2, transcendentals=0),
        name="near_terms",
    )(count, mats, *rows)


def shift(value, steps):
    return lax.ppermute(value, AXES, [(i, (i + steps) % DEV) for i in range(DEV)])


def on_device(potentials, leaf_to_panel, density, corrections, correction_rows, correction_cols, block_count):
    me = lax.axis_index(AXES).astype(I32).reshape(1)
    live = jnp.arange(SLOTS) < block_count[0]
    ask = jnp.stack([jnp.tile(correction_cols, 4), jnp.tile(jnp.where(live, correction_rows, -1), 4)])
    asks = (ask, shift(ask, 1), shift(ask, -1))
    message = pack(leaf_to_panel, potentials)
    own, for_prev, for_next, message = fetch(me, asks, density, message)
    rows = (own, shift(for_next, 1), shift(for_prev, -1))
    arrived = lax.all_to_all(
        message.reshape(DEV, LINES, 1, 128), AXES, split_axis=0, concat_axis=0, tiled=True
    ).reshape(DEV * LINES, 128)
    term = make_terms(block_count, corrections, rows)
    terms = (term, shift(term, 1), shift(term, -1))
    return place(me, arrived, terms, asks)


def solution(mesh):
    rows = P(AXES, None)
    flat = P(AXES)
    return jax.shard_map(
        on_device,
        mesh=mesh,
        in_specs=(rows, flat, rows, P(AXES, None, None), flat, flat, flat),
        out_specs=rows,
        check_vma=False,
    )
```

```python
import functools

import jax
import jax.numpy as jnp
from jax import lax
from jax.experimental import pallas as pl
from jax.experimental.pallas import tpu as pltpu
from jax.sharding import PartitionSpec as P

AXES = ("leaf", "panel")
DEV = 128
CAP = 16
ROWS = 1024
BW = 384
TILES = BW // 128
LINES = CAP // 2 * TILES + 1
SLOTS = 32
TOTAL = DEV * ROWS
F32, BF16, I32 = jnp.float32, jnp.bfloat16, jnp.int32
NT = (((1,), (1,)), ((), ()))
VMEM = pl.BlockSpec(memory_space=pltpu.VMEM)
SMEM = pl.BlockSpec(memory_space=pltpu.SMEM)
HBM = pl.BlockSpec(memory_space=pltpu.HBM)


def iota(shape, dim):
    return lax.broadcasted_iota(I32, shape, dim)


def one_hot(mask):
    return jnp.where(mask, 1.0, 0.0).astype(BF16)


def row16(row):
    return jnp.broadcast_to(row, (16, 128)).astype(BF16)[None]


def times_row(block, row):
    return (block.reshape(8, 16, 128) * row16(row)).reshape(128, 128)


def mm(a, b):
    return jnp.dot(a, b, preferred_element_type=F32)


def pack_kernel(map_hbm, pot_hbm, out_hbm, place, pot, msg, sel, dig, head, sems):
    get_map = pltpu.make_async_copy(map_hbm, place, sems.at[0])
    get_map.start()
    get_pot = []
    for g in range(4):
        rows = pl.ds(g * 256, 256)
        get_pot.append(pltpu.make_async_copy(pot_hbm.at[rows], pot.at[rows], sems.at[1 + g]))
        get_pot[g].start()
    get_map.wait()

    dest, label = place[...] >> 10, (place[...] & (ROWS - 1)) + 1
    sub = iota((128, 128), 0)
    before = jnp.concatenate([one_hot(sub < iota((128, 128), 1)), one_hot(sub >= 0)], axis=1)
    hits = [dest[b : b + 1, :] == sub for b in range(8)]
    hot = [one_hot(h) for h in hits]
    counts = mm(jnp.concatenate(hot, axis=0), before)
    carry = jnp.zeros((128, 128), F32)
    ranks = []
    for b in range(8):
        part = counts[b * 128 : b * 128 + 128]
        ranks.append(jnp.sum(jnp.where(hits[b], part[:, :128] + carry, 0.0), axis=0, keepdims=True))
        carry = carry + part[:, 128:]
    low = sub & (CAP - 1)
    ranked = []
    for b in range(8):
        lanes = pl.ds(b * 128, 128)
        for c in range(CAP):
            block = times_row(hot[b], jnp.where(ranks[b] == c, 1.0, 0.0))
            for g in range(8):
                sel[pl.ds(g * 256 + c * 16, 16), lanes] = block[g * 16 : g * 16 + 16]
        ranked.append(one_hot(ranks[b].astype(I32) == low))

    for g in range(8):
        if g % 2 == 0:
            get_pot[g // 2].wait()
        rows = pl.ds(g * 128, 128)
        x = pot[rows, :]
        top = jnp.max(jnp.abs(x), axis=1, keepdims=True)
        step = jnp.maximum(top * (1.0 / 32766.0), 2.0**-100)
        expo = jnp.floor(jnp.log2(step) + 1e-3)
        power = jnp.exp2(expo).astype(BF16).astype(F32)
        mant = jnp.maximum(jnp.ceil((step / power - 1.0) * 64.0), 0.0)
        scale = power * (1.0 + mant * (1.0 / 64.0))
        q = jnp.clip(jnp.round(x * (1.0 / scale)), -32767.0, 32767.0)
        hi = jnp.floor(q * (1.0 / 256.0))
        lo = q - hi * 256.0
        for n in range(TILES):
            dig[rows, pl.ds(n * 256, 128)] = hi[:, n * 128 : n * 128 + 128].astype(BF16)
            dig[rows, pl.ds(n * 256 + 128, 128)] = lo[:, n * 128 : n * 128 + 128].astype(BF16)
        lane = iota((128, 128), 1)
        head[rows, :] = jnp.where(lane == 0, expo + 128.0, jnp.where(lane == 1, mant, 0.0)).astype(BF16)
    eye = one_hot(iota((16, 128), 0) == iota((16, 128), 1))
    codes = lax.dot_general(eye, head[...], NT, preferred_element_type=F32)

    digits = [[], [], [], []]
    for b in range(8):
        lab = label[b : b + 1, :]
        cols = slice(b * 128, b * 128 + 128)
        for k, row in enumerate(
            ((lab >> 7).astype(F32), (lab & 127).astype(F32), codes[0:1, cols], codes[1:2, cols])
        ):
            digits[k].append(times_row(hot[b], row))
    left = jnp.concatenate([jnp.concatenate(d, axis=1) for d in digits], axis=0)
    meta = lax.dot_general(left, jnp.concatenate(ranked, axis=1), NT, preferred_element_type=F32).astype(I32)
    words = jnp.where(
        iota((128, 128), 1) < CAP, meta[0:128] * 128 + meta[128:256], meta[256:384] * 128 + meta[384:512]
    )
    msg[pl.ds(LINES - 1, DEV, stride=LINES), :] = words

    put = []
    for g in range(8):
        for n in range(TILES):
            both = mm(sel[pl.ds(g * 256, 256), :], dig[:, pl.ds(n * 256, 256)])
            q = (both[:, :128] * 256.0 + both[:, 128:]).astype(I32)
            w = (q[128:] << 16) | (q[:128] & 0xFFFF)
            for r in range(8):
                msg[pl.ds(g * 16 * LINES + n * 8 + r, 16, stride=LINES), :] = w[r * 16 : r * 16 + 16]
        lines = pl.ds(g * 16 * LINES, 16 * LINES)
        put.append(pltpu.make_async_copy(msg.at[lines], out_hbm.at[lines], sems.at[5 + g]))
        put[g].start()
    for copy in put:
        copy.wait()


def pack(leaf_to_panel, potentials):
    return pl.pallas_call(
        pack_kernel,
        out_shape=jax.ShapeDtypeStruct((DEV * LINES, 128), I32),
        in_specs=[HBM, HBM],
        out_specs=HBM,
        scratch_shapes=[
            pltpu.VMEM((8, 128), I32),
            pltpu.VMEM((ROWS, BW), F32),
            pltpu.VMEM((DEV * LINES, 128), I32),
            pltpu.VMEM((DEV * CAP, ROWS), BF16),
            pltpu.VMEM((ROWS, 2 * BW), BF16),
            pltpu.VMEM((ROWS, 128), BF16),
            pltpu.SemaphoreType.DMA((13,)),
        ],
        compiler_params=pltpu.CompilerParams(vmem_limit_bytes=60 * 2**20),
        cost_estimate=pl.CostEstimate(flops=2 * DEV * CAP * ROWS * 2 * BW, bytes_accessed=4 * 2**20, transcendentals=0),
        name="pack_rows",
    )(leaf_to_panel.reshape(8, 128), potentials)


def place_kernel(me_ref, msg_ref, own_ref, prev_ref, next_ref, out_ref, sel, dig):
    heads = jnp.transpose(msg_ref[pl.ds(LINES - 1, DEV, stride=LINES), :].astype(F32)).astype(I32)
    target = heads[0:CAP] - 1
    code = heads[CAP : 2 * CAP]
    high, low = target >> 7, target & 127
    scale = jnp.exp2((code >> 7).astype(F32) - 128.0).astype(BF16).astype(F32)
    scale = scale * (1.0 + (code & 127).astype(F32) * (1.0 / 64.0))
    sub = iota((128, 128), 0)
    for c in range(CAP):
        hot = one_hot(low[c : c + 1] == sub)
        for g in range(8):
            row = jnp.where(high[c : c + 1] == g, scale[c : c + 1], 0.0)
            sel[pl.ds(g * 128, 128), pl.ds(c * 128, 128)] = times_row(hot, row)
    lane = iota((1, 128), 1)
    base = me_ref[0] * ROWS
    own, prev, following = (ref[SLOTS : SLOTS + 1, 0:128] for ref in (own_ref, prev_ref, next_ref))
    rows = jnp.where(lane < SLOTS, own, jnp.where(lane < 2 * SLOTS, prev, following)).astype(I32)
    target = jnp.where((rows < 0) | (lane >= 3 * SLOTS), -1, (rows - base) & (TOTAL - 1))
    for g in range(8):
        hot = one_hot(target - g * 128 == sub)
        sel[pl.ds(g * 128, 128), pl.ds(CAP * 128, 128)] = hot
        sel[pl.ds(g * 128, 128), pl.ds(CAP * 128 + 128, 128)] = hot
    near = jnp.concatenate([own_ref[0:SLOTS], prev_ref[0:SLOTS], next_ref[0:SLOTS], jnp.zeros((SLOTS, BW), F32)], axis=0)
    first = near.astype(BF16)
    second = (near - first.astype(F32)).astype(BF16)
    blank = jnp.zeros((256, 128), BF16)
    for n in range(TILES):
        for r in range(8):
            w = msg_ref[pl.ds(n * 8 + r, DEV, stride=LINES), :]
            for c, hi, lo in ((r, (w << 16) >> 24, w & 255), (r + 8, w >> 24, (w >> 16) & 255)):
                dig[pl.ds(c * 128, 128), pl.ds(n * 256, 128)] = hi.astype(F32).astype(BF16)
                dig[pl.ds(c * 128, 128), pl.ds(n * 256 + 128, 128)] = lo.astype(F32).astype(BF16)
        dig[pl.ds(CAP * 128, 256), pl.ds(n * 256, 128)] = blank
        dig[pl.ds(CAP * 128, 128), pl.ds(n * 256 + 128, 128)] = first[:, n * 128 : n * 128 + 128]
        dig[pl.ds(CAP * 128 + 128, 128), pl.ds(n * 256 + 128, 128)] = second[:, n * 128 : n * 128 + 128]
        for g in range(4):
            both = mm(sel[pl.ds(g * 256, 256), :], dig[:, pl.ds(n * 256, 256)])
            out_ref[pl.ds(g * 256, 256), pl.ds(n * 128, 128)] = both[:, :128] * 256.0 + both[:, 128:]


def place(me, arrived, terms):
    return pl.pallas_call(
        place_kernel,
        out_shape=jax.ShapeDtypeStruct((ROWS, BW), F32),
        in_specs=[SMEM] + [VMEM] * 4,
        out_specs=VMEM,
        scratch_shapes=[
            pltpu.VMEM((ROWS, CAP * 128 + 256), BF16),
            pltpu.VMEM((CAP * 128 + 256, 2 * BW), BF16),
        ],
        compiler_params=pltpu.CompilerParams(vmem_limit_bytes=40 * 2**20),
        cost_estimate=pl.CostEstimate(flops=2 * DEV * CAP * ROWS * 2 * BW, bytes_accessed=4 * 2**20, transcendentals=0),
        name="place_rows",
    )(me, arrived, *terms)


STEP = 4


def term_kernel(me_ref, count_ref, mats_ref, cols_ref, rows_ref, own_ref, prev_ref, next_ref, out_ref, acc, vecs):
    step = pl.program_id(0)

    @pl.when(step == 0)
    def _():
        acc[...] = jnp.zeros_like(acc)
        at = ((cols_ref[...] - (me_ref[0] - 1) * ROWS) & (TOTAL - 1)).astype(F32)
        at = jnp.transpose(jnp.broadcast_to(at, (128, 128)))[0:SLOTS].astype(I32)
        lane = iota((SLOTS, 128), 1)
        got = jnp.zeros((SLOTS, BW), F32)
        for k, ref in enumerate((prev_ref, own_ref, next_ref)):
            hot = [one_hot(at - (k * ROWS + b * 128) == lane) for b in range(8)]
            got = got + mm(jnp.concatenate(hot, axis=1), ref[...])
        vecs[...] = jnp.concatenate([got, jnp.zeros((128 - SLOTS, BW), F32)], axis=0).astype(BF16)

    lane = iota((BW, 128), 1)
    total = acc[...]
    for k in range(STEP):
        prod = lax.dot_general(mats_ref[k], vecs[...], NT, preferred_element_type=F32)
        total = jnp.where(lane == step * STEP + k, prod, total)
    acc[...] = total

    @pl.when(step == SLOTS // STEP - 1)
    def _():
        live = iota((SLOTS, BW), 0) < count_ref[0]
        out_ref[0:SLOTS, :] = jnp.where(live, jnp.transpose(acc[...])[0:SLOTS], 0.0)
        slot = iota((1, 128), 1) & (SLOTS - 1)
        rows = jnp.where(slot < count_ref[0], rows_ref[...], -1).astype(F32)
        for n in range(TILES):
            out_ref[SLOTS : SLOTS + 8, n * 128 : n * 128 + 128] = jnp.broadcast_to(rows, (8, 128))


def make_terms(me, count, mats, cols, rows, blocks):
    def whole(rows, width):
        return pl.BlockSpec((rows, width), lambda i: (0, 0))

    return pl.pallas_call(
        term_kernel,
        grid=(SLOTS // STEP,),
        out_shape=jax.ShapeDtypeStruct((SLOTS + 8, BW), F32),
        in_specs=[SMEM, SMEM, pl.BlockSpec((STEP, BW, BW), lambda i: (i, 0, 0))]
        + [whole(1, 128)] * 2
        + [whole(ROWS, BW)] * 3,
        out_specs=whole(SLOTS + 8, BW),
        scratch_shapes=[pltpu.VMEM((BW, 128), F32), pltpu.VMEM((128, BW), BF16)],
        compiler_params=pltpu.CompilerParams(vmem_limit_bytes=30 * 2**20),
        cost_estimate=pl.CostEstimate(flops=10**10, bytes_accessed=SLOTS * BW * BW * 2, transcendentals=0),
        name="near_terms",
    )(me, count, mats, cols, rows, *blocks)


def shift(value, steps):
    return lax.ppermute(value, AXES, [(i, (i + steps) % DEV) for i in range(DEV)])


def on_device(potentials, leaf_to_panel, density, corrections, correction_rows, correction_cols, block_count):
    me = lax.axis_index(AXES).astype(I32).reshape(1)
    blocks = (density, shift(density, 1), shift(density, -1))
    message = pack(leaf_to_panel, potentials)
    arrived = lax.all_to_all(
        message.reshape(DEV, LINES, 1, 128), AXES, split_axis=0, concat_axis=0, tiled=True
    ).reshape(DEV * LINES, 128)
    cols, rows = (jnp.tile(x, 128 // SLOTS).reshape(1, 128) for x in (correction_cols, correction_rows))
    term = make_terms(me, block_count, corrections, cols, rows, blocks)
    terms = (term, shift(term, 1), shift(term, -1))
    return place(me, arrived, terms)


def solution(mesh):
    rows = P(AXES, None)
    flat = P(AXES)
    return jax.shard_map(
        on_device,
        mesh=mesh,
        in_specs=(rows, flat, rows, P(AXES, None, None), flat, flat, flat),
        out_specs=rows,
        check_vma=False,
    )
```

```python
import functools

import jax
import jax.numpy as jnp
from jax import lax
from jax.experimental import pallas as pl
from jax.experimental.pallas import tpu as pltpu
from jax.sharding import PartitionSpec as P

AXES = ("leaf", "panel")
DEV = 128
CAP = 16
ROWS = 1024
BW = 384
TILES = BW // 128
LINES = CAP // 2 * TILES + 1
SLOTS = 32
TOTAL = DEV * ROWS
F32, BF16, I32 = jnp.float32, jnp.bfloat16, jnp.int32
NT = (((1,), (1,)), ((), ()))
VMEM = pl.BlockSpec(memory_space=pltpu.VMEM)
SMEM = pl.BlockSpec(memory_space=pltpu.SMEM)
HBM = pl.BlockSpec(memory_space=pltpu.HBM)


def iota(shape, dim):
    return lax.broadcasted_iota(I32, shape, dim)


def one_hot(mask):
    return jnp.where(mask, 1.0, 0.0).astype(BF16)


def row16(row):
    return jnp.broadcast_to(row, (16, 128)).astype(BF16)[None]


def times_row(block, row):
    return (block.reshape(8, 16, 128) * row16(row)).reshape(128, 128)


def mm(a, b):
    return jnp.dot(a, b, preferred_element_type=F32)


def pack_kernel(map_hbm, pot_hbm, out_hbm, place, pot, msg, sel, dig, head, sems):
    get_map = pltpu.make_async_copy(map_hbm, place, sems.at[0])
    get_map.start()
    get_pot = []
    for g in range(4):
        rows = pl.ds(g * 256, 256)
        get_pot.append(pltpu.make_async_copy(pot_hbm.at[rows], pot.at[rows], sems.at[1 + g]))
        get_pot[g].start()
    get_map.wait()

    dest, label = place[...] >> 10, (place[...] & (ROWS - 1)) + 1
    sub = iota((128, 128), 0)
    before = jnp.concatenate([one_hot(sub < iota((128, 128), 1)), one_hot(sub >= 0)], axis=1)
    hits = [dest[b : b + 1, :] == sub for b in range(8)]
    hot = [one_hot(h) for h in hits]
    counts = mm(jnp.concatenate(hot, axis=0), before)
    carry = jnp.zeros((128, 128), F32)
    ranks = []
    for b in range(8):
        part = counts[b * 128 : b * 128 + 128]
        ranks.append(jnp.sum(jnp.where(hits[b], part[:, :128] + carry, 0.0), axis=0, keepdims=True))
        carry = carry + part[:, 128:]
    low = sub & (CAP - 1)
    ranked = []
    for b in range(8):
        lanes = pl.ds(b * 128, 128)
        for c in range(CAP):
            block = times_row(hot[b], jnp.where(ranks[b] == c, 1.0, 0.0))
            for g in range(8):
                sel[pl.ds(g * 256 + c * 16, 16), lanes] = block[g * 16 : g * 16 + 16]
        ranked.append(one_hot(ranks[b].astype(I32) == low))

    for g in range(8):
        if g % 2 == 0:
            get_pot[g // 2].wait()
        rows = pl.ds(g * 128, 128)
        x = pot[rows, :]
        top = jnp.max(jnp.abs(x), axis=1, keepdims=True)
        step = jnp.maximum(top * (1.0 / 32766.0), 2.0**-100)
        expo = jnp.floor(jnp.log2(step) + 1e-3)
        power = jnp.exp2(expo).astype(BF16).astype(F32)
        mant = jnp.maximum(jnp.ceil((step / power - 1.0) * 64.0), 0.0)
        scale = power * (1.0 + mant * (1.0 / 64.0))
        q = jnp.clip(jnp.round(x * (1.0 / scale)), -32767.0, 32767.0)
        hi = jnp.floor(q * (1.0 / 256.0))
        lo = q - hi * 256.0
        for n in range(TILES):
            dig[rows, pl.ds(n * 256, 128)] = hi[:, n * 128 : n * 128 + 128].astype(BF16)
            dig[rows, pl.ds(n * 256 + 128, 128)] = lo[:, n * 128 : n * 128 + 128].astype(BF16)
        lane = iota((128, 128), 1)
        head[rows, :] = jnp.where(lane == 0, expo + 128.0, jnp.where(lane == 1, mant, 0.0)).astype(BF16)
    eye = one_hot(iota((16, 128), 0) == iota((16, 128), 1))
    codes = lax.dot_general(eye, head[...], NT, preferred_element_type=F32)

    digits = [[], [], [], []]
    for b in range(8):
        lab = label[b : b + 1, :]
        cols = slice(b * 128, b * 128 + 128)
        for k, row in enumerate(
            ((lab >> 7).astype(F32), (lab & 127).astype(F32), codes[0:1, cols], codes[1:2, cols])
        ):
            digits[k].append(times_row(hot[b], row))
    left = jnp.concatenate([jnp.concatenate(d, axis=1) for d in digits], axis=0)
    meta = lax.dot_general(left, jnp.concatenate(ranked, axis=1), NT, preferred_element_type=F32).astype(I32)
    words = jnp.where(
        iota((128, 128), 1) < CAP, meta[0:128] * 128 + meta[128:256], meta[256:384] * 128 + meta[384:512]
    )
    msg[pl.ds(LINES - 1, DEV, stride=LINES), :] = words

    put = []
    for g in range(8):
        for n in range(TILES):
            both = mm(sel[pl.ds(g * 256, 256), :], dig[:, pl.ds(n * 256, 256)])
            q = (both[:, :128] * 256.0 + both[:, 128:]).astype(I32)
            w = (q[128:] << 16) | (q[:128] & 0xFFFF)
            for r in range(8):
                msg[pl.ds(g * 16 * LINES + n * 8 + r, 16, stride=LINES), :] = w[r * 16 : r * 16 + 16]
        lines = pl.ds(g * 16 * LINES, 16 * LINES)
        put.append(pltpu.make_async_copy(msg.at[lines], out_hbm.at[lines], sems.at[5 + g]))
        put[g].start()
    for copy in put:
        copy.wait()


def pack(leaf_to_panel, potentials):
    return pl.pallas_call(
        pack_kernel,
        out_shape=jax.ShapeDtypeStruct((DEV * LINES, 128), I32),
        in_specs=[HBM, HBM],
        out_specs=HBM,
        scratch_shapes=[
            pltpu.VMEM((8, 128), I32),
            pltpu.VMEM((ROWS, BW), F32),
            pltpu.VMEM((DEV * LINES, 128), I32),
            pltpu.VMEM((DEV * CAP, ROWS), BF16),
            pltpu.VMEM((ROWS, 2 * BW), BF16),
            pltpu.VMEM((ROWS, 128), BF16),
            pltpu.SemaphoreType.DMA((13,)),
        ],
        compiler_params=pltpu.CompilerParams(vmem_limit_bytes=60 * 2**20),
        cost_estimate=pl.CostEstimate(flops=2 * DEV * CAP * ROWS * 2 * BW, bytes_accessed=4 * 2**20, transcendentals=0),
        name="pack_rows",
    )(leaf_to_panel.reshape(8, 128), potentials)


def place_kernel(me_ref, msg_ref, own_ref, near_ref, far_ref, out_ref, sel, dig):
    heads = jnp.transpose(msg_ref[pl.ds(LINES - 1, DEV, stride=LINES), :].astype(F32)).astype(I32)
    target = heads[0:CAP] - 1
    code = heads[CAP : 2 * CAP]
    high, low = target >> 7, target & 127
    scale = jnp.exp2((code >> 7).astype(F32) - 128.0).astype(BF16).astype(F32)
    scale = scale * (1.0 + (code & 127).astype(F32) * (1.0 / 64.0))
    sub = iota((128, 128), 0)
    for c in range(CAP):
        hot = one_hot(low[c : c + 1] == sub)
        for g in range(8):
            row = jnp.where(high[c : c + 1] == g, scale[c : c + 1], 0.0)
            sel[pl.ds(g * 128, 128), pl.ds(c * 128, 128)] = times_row(hot, row)
    lane = iota((1, 128), 1)
    base = me_ref[0] * ROWS
    own, adjacent, other = (ref[SLOTS : SLOTS + 1, 0:128] for ref in (own_ref, near_ref, far_ref))
    rows = jnp.where(lane < SLOTS, own, jnp.where(lane < 2 * SLOTS, adjacent, other)).astype(I32)
    target = jnp.where((rows < 0) | (lane >= 3 * SLOTS), -1, (rows - base) & (TOTAL - 1))
    for g in range(8):
        hot = one_hot(target - g * 128 == sub)
        sel[pl.ds(g * 128, 128), pl.ds(CAP * 128, 128)] = hot
        sel[pl.ds(g * 128, 128), pl.ds(CAP * 128 + 128, 128)] = hot
    near = jnp.concatenate([own_ref[0:SLOTS], near_ref[0:SLOTS], far_ref[0:SLOTS], jnp.zeros((SLOTS, BW), F32)], axis=0)
    first = near.astype(BF16)
    second = (near - first.astype(F32)).astype(BF16)
    blank = jnp.zeros((256, 128), BF16)
    for n in range(TILES):
        for r in range(8):
            w = msg_ref[pl.ds(n * 8 + r, DEV, stride=LINES), :]
            for c, hi, lo in ((r, (w << 16) >> 24, w & 255), (r + 8, w >> 24, (w >> 16) & 255)):
                dig[pl.ds(c * 128, 128), pl.ds(n * 256, 128)] = hi.astype(F32).astype(BF16)
                dig[pl.ds(c * 128, 128), pl.ds(n * 256 + 128, 128)] = lo.astype(F32).astype(BF16)
        dig[pl.ds(CAP * 128, 256), pl.ds(n * 256, 128)] = blank
        dig[pl.ds(CAP * 128, 128), pl.ds(n * 256 + 128, 128)] = first[:, n * 128 : n * 128 + 128]
        dig[pl.ds(CAP * 128 + 128, 128), pl.ds(n * 256 + 128, 128)] = second[:, n * 128 : n * 128 + 128]
        for g in range(4):
            both = mm(sel[pl.ds(g * 256, 256), :], dig[:, pl.ds(n * 256, 256)])
            out_ref[pl.ds(g * 256, 256), pl.ds(n * 128, 128)] = both[:, :128] * 256.0 + both[:, 128:]


def place(me, arrived, terms):
    return pl.pallas_call(
        place_kernel,
        out_shape=jax.ShapeDtypeStruct((ROWS, BW), F32),
        in_specs=[SMEM] + [VMEM] * 4,
        out_specs=VMEM,
        scratch_shapes=[
            pltpu.VMEM((ROWS, CAP * 128 + 256), BF16),
            pltpu.VMEM((CAP * 128 + 256, 2 * BW), BF16),
        ],
        compiler_params=pltpu.CompilerParams(vmem_limit_bytes=40 * 2**20),
        cost_estimate=pl.CostEstimate(flops=2 * DEV * CAP * ROWS * 2 * BW, bytes_accessed=4 * 2**20, transcendentals=0),
        name="place_rows",
    )(me, arrived, *terms)


def fetch_kernel(me_ref, own_cols, near_cols, far_cols, density_ref, msg_ref, own_ref, near_ref, far_ref, out_ref):
    base = me_ref[0] * ROWS
    cols = jnp.concatenate([own_cols[...], near_cols[...], far_cols[...], own_cols[...]], axis=1)
    at = ((cols - base) & (TOTAL - 1)).astype(F32)
    at = jnp.transpose(jnp.broadcast_to(at, (128, 128)))[0 : 3 * SLOTS].astype(I32)
    lane = iota((3 * SLOTS, 128), 1)
    hot = jnp.concatenate([one_hot(at - b * 128 == lane) for b in range(8)], axis=1)
    got = mm(hot, density_ref[...]).astype(BF16)
    own_ref[...] = got[0:SLOTS]
    near_ref[...] = got[SLOTS : 2 * SLOTS]
    far_ref[...] = got[2 * SLOTS :]


def fetch(me, cols, density, message):
    rows = jax.ShapeDtypeStruct((SLOTS, BW), BF16)
    return pl.pallas_call(
        fetch_kernel,
        out_shape=(rows, rows, rows, jax.ShapeDtypeStruct(message.shape, message.dtype)),
        in_specs=[SMEM] + [VMEM] * 4 + [HBM],
        out_specs=(VMEM, VMEM, VMEM, HBM),
        input_output_aliases={5: 3},
        compiler_params=pltpu.CompilerParams(vmem_limit_bytes=105 * 2**19),
        cost_estimate=pl.CostEstimate(flops=10**8, bytes_accessed=2**20, transcendentals=0),
        name="fetch_density",
    )(me, *(x.reshape(1, SLOTS) for x in cols), density, message)


STEP = 4


def term_kernel(count_ref, mats_ref, targets_ref, own_ref, near_ref, far_ref, out_ref, acc, vecs):
    step = pl.program_id(0)

    @pl.when(step == 0)
    def _():
        acc[...] = jnp.zeros_like(acc)
        got = own_ref[...].astype(F32) + near_ref[...].astype(F32) + far_ref[...].astype(F32)
        vecs[...] = jnp.concatenate([got, jnp.zeros((128 - SLOTS, BW), F32)], axis=0).astype(BF16)

    lane = iota((BW, 128), 1)
    total = acc[...]
    for k in range(STEP):
        prod = lax.dot_general(mats_ref[k], vecs[...], NT, preferred_element_type=F32)
        total = jnp.where(lane == step * STEP + k, prod, total)
    acc[...] = total

    @pl.when(step == SLOTS // STEP - 1)
    def _():
        live = iota((SLOTS, BW), 0) < count_ref[0]
        out_ref[0:SLOTS, :] = jnp.where(live, jnp.transpose(acc[...])[0:SLOTS], 0.0)
        slot = iota((1, 128), 1) & (SLOTS - 1)
        rows = jnp.where(slot < count_ref[0], targets_ref[...], -1).astype(F32)
        for n in range(TILES):
            out_ref[SLOTS : SLOTS + 8, n * 128 : n * 128 + 128] = jnp.broadcast_to(rows, (8, 128))


def make_terms(count, mats, targets, rows):
    def whole(rows, width):
        return pl.BlockSpec((rows, width), lambda i: (0, 0))

    return pl.pallas_call(
        term_kernel,
        grid=(SLOTS // STEP,),
        out_shape=jax.ShapeDtypeStruct((SLOTS + 8, BW), F32),
        in_specs=[SMEM, pl.BlockSpec((STEP, BW, BW), lambda i: (i, 0, 0)), whole(1, 128)] + [whole(SLOTS, BW)] * 3,
        out_specs=whole(SLOTS + 8, BW),
        scratch_shapes=[pltpu.VMEM((BW, 128), F32), pltpu.VMEM((128, BW), BF16)],
        compiler_params=pltpu.CompilerParams(vmem_limit_bytes=20 * 2**20),
        cost_estimate=pl.CostEstimate(flops=6 * 10**10, bytes_accessed=SLOTS * BW * BW * 2, transcendentals=0),
        name="near_terms",
    )(count, mats, targets, *rows)


def swap_near(value):
    return lax.ppermute(value, AXES, [(i, i ^ 1) for i in range(DEV)])


def swap_far(value):
    return lax.ppermute(value, AXES, [(i, (i - 1 + 2 * (i % 2)) % DEV) for i in range(DEV)])


def on_device(potentials, leaf_to_panel, density, corrections, correction_rows, correction_cols, block_count):
    me = lax.axis_index(AXES).astype(I32).reshape(1)
    cols = (correction_cols, swap_near(correction_cols), swap_far(correction_cols))
    message = pack(leaf_to_panel, potentials)
    own, for_near, for_far, message = fetch(me, cols, density, message)
    rows = (own, swap_near(for_near), swap_far(for_far))
    arrived = lax.all_to_all(
        message.reshape(DEV, LINES, 1, 128), AXES, split_axis=0, concat_axis=0, tiled=True
    ).reshape(DEV * LINES, 128)
    targets = jnp.tile(correction_rows, 128 // SLOTS).reshape(1, 128)
    term = make_terms(block_count, corrections, targets, rows)
    terms = (term, swap_near(term), swap_far(term))
    return place(me, arrived, terms)


def solution(mesh):
    rows = P(AXES, None)
    flat = P(AXES)
    return jax.shard_map(
        on_device,
        mesh=mesh,
        in_specs=(rows, flat, rows, P(AXES, None, None), flat, flat, flat),
        out_specs=rows,
        check_vma=False,
    )
```

```python
import functools

import jax
import jax.numpy as jnp
from jax import lax
from jax.experimental import pallas as pl
from jax.experimental.pallas import tpu as pltpu
from jax.sharding import PartitionSpec as P

AXES = ("leaf", "panel")
DEV = 128
CAP = 16
HALF = CAP // 2
ROWS = 1024
BW = 384
TILES = BW // 128
LINES = HALF * TILES + 1
SLOTS = 32
TOTAL = DEV * ROWS
F32, BF16, I32 = jnp.float32, jnp.bfloat16, jnp.int32
NT = (((1,), (1,)), ((), ()))
VMEM = pl.BlockSpec(memory_space=pltpu.VMEM)
SMEM = pl.BlockSpec(memory_space=pltpu.SMEM)
HBM = pl.BlockSpec(memory_space=pltpu.HBM)


def iota(shape, dim):
    return lax.broadcasted_iota(I32, shape, dim)


def one_hot(mask):
    return jnp.where(mask, 1.0, 0.0).astype(BF16)


def row16(row):
    return jnp.broadcast_to(row, (16, 128)).astype(BF16)[None]


def times_row(block, row):
    return (block.reshape(8, 16, 128) * row16(row)).reshape(128, 128)


def mm(a, b):
    return jnp.dot(a, b, preferred_element_type=F32)


def pack_kernel(map_hbm, pot_hbm, out_hbm, place, pot, msg, sel, dig, head, sems):
    get_map = pltpu.make_async_copy(map_hbm, place, sems.at[0])
    get_map.start()
    get_pot = []
    for g in range(4):
        rows = pl.ds(g * 256, 256)
        get_pot.append(pltpu.make_async_copy(pot_hbm.at[rows], pot.at[rows], sems.at[1 + g]))
        get_pot[g].start()
    get_map.wait()

    dest, label = place[...] >> 10, (place[...] & (ROWS - 1)) + 1
    sub = iota((128, 128), 0)
    before = jnp.concatenate([one_hot(sub < iota((128, 128), 1)), one_hot(sub >= 0)], axis=1)
    hits = [dest[b : b + 1, :] == sub for b in range(8)]
    hot = [one_hot(h) for h in hits]
    counts = mm(jnp.concatenate(hot, axis=0), before)
    carry = jnp.zeros((128, 128), F32)
    ranks = []
    for b in range(8):
        part = counts[b * 128 : b * 128 + 128]
        ranks.append(jnp.sum(jnp.where(hits[b], part[:, :128] + carry, 0.0), axis=0, keepdims=True))
        carry = carry + part[:, 128:]
    low = sub & (CAP - 1)
    ranked = []
    for b in range(8):
        lanes = pl.ds(b * 128, 128)
        for r in range(HALF):
            weight = jnp.where(ranks[b] == r, 1.0, jnp.where(ranks[b] == r + HALF, 256.0, 0.0))
            block = times_row(hot[b], weight)
            for g in range(4):
                sel[pl.ds(g * 256 + r * 32, 32), lanes] = block[g * 32 : g * 32 + 32]
        ranked.append(one_hot(ranks[b].astype(I32) == low))

    for g in range(8):
        if g % 2 == 0:
            get_pot[g // 2].wait()
        rows = pl.ds(g * 128, 128)
        x = pot[rows, :]
        top = jnp.max(jnp.abs(x), axis=1, keepdims=True)
        step = jnp.maximum(top * (1.0 / 32766.0), 2.0**-100)
        expo = jnp.floor(jnp.log2(step) + 1e-3)
        power = jnp.exp2(expo).astype(BF16).astype(F32)
        mant = jnp.maximum(jnp.ceil((step / power - 1.0) * 64.0), 0.0)
        scale = power * (1.0 + mant * (1.0 / 64.0))
        q = jnp.clip(jnp.round(x * (1.0 / scale)), -32767.0, 32767.0)
        hi = jnp.floor(q * (1.0 / 256.0))
        lo = q - hi * 256.0
        hi = hi + 128.0
        for n in range(TILES):
            dig[rows, pl.ds(n * 256, 128)] = hi[:, n * 128 : n * 128 + 128].astype(BF16)
            dig[rows, pl.ds(n * 256 + 128, 128)] = lo[:, n * 128 : n * 128 + 128].astype(BF16)
        lane = iota((128, 128), 1)
        head[rows, :] = jnp.where(lane == 0, expo + 128.0, jnp.where(lane == 1, mant, 0.0)).astype(BF16)
    eye = one_hot(iota((16, 128), 0) == iota((16, 128), 1))
    codes = lax.dot_general(eye, head[...], NT, preferred_element_type=F32)

    digits = [[], [], [], []]
    for b in range(8):
        lab = label[b : b + 1, :]
        cols = slice(b * 128, b * 128 + 128)
        for k, row in enumerate(
            ((lab >> 7).astype(F32), (lab & 127).astype(F32), codes[0:1, cols], codes[1:2, cols])
        ):
            digits[k].append(times_row(hot[b], row))
    left = jnp.concatenate([jnp.concatenate(d, axis=1) for d in digits], axis=0)
    meta = lax.dot_general(left, jnp.concatenate(ranked, axis=1), NT, preferred_element_type=F32).astype(I32)
    words = jnp.where(
        iota((128, 128), 1) < CAP, meta[0:128] * 128 + meta[128:256], meta[256:384] * 128 + meta[384:512]
    )
    msg[pl.ds(LINES - 1, DEV, stride=LINES), :] = words

    put = []
    for g in range(4):
        for n in range(TILES):
            both = mm(sel[pl.ds(g * 256, 256), :], dig[:, pl.ds(n * 256, 256)]).astype(I32)
            w = (both[:, :128] << 16) | both[:, 128:]
            for r in range(HALF):
                msg[pl.ds(g * 32 * LINES + n * HALF + r, 32, stride=LINES), :] = w[r * 32 : r * 32 + 32]
        lines = pl.ds(g * 32 * LINES, 32 * LINES)
        put.append(pltpu.make_async_copy(msg.at[lines], out_hbm.at[lines], sems.at[5 + g]))
        put[g].start()
    for copy in put:
        copy.wait()


def pack(leaf_to_panel, potentials):
    return pl.pallas_call(
        pack_kernel,
        out_shape=jax.ShapeDtypeStruct((DEV * LINES, 128), I32),
        in_specs=[HBM, HBM],
        out_specs=HBM,
        scratch_shapes=[
            pltpu.VMEM((8, 128), I32),
            pltpu.VMEM((ROWS, BW), F32),
            pltpu.VMEM((DEV * LINES, 128), I32),
            pltpu.VMEM((DEV * HALF, ROWS), BF16),
            pltpu.VMEM((ROWS, 2 * BW), BF16),
            pltpu.VMEM((ROWS, 128), BF16),
            pltpu.SemaphoreType.DMA((9,)),
        ],
        compiler_params=pltpu.CompilerParams(vmem_limit_bytes=60 * 2**20),
        cost_estimate=pl.CostEstimate(flops=2 * DEV * CAP * ROWS * 2 * BW, bytes_accessed=4 * 2**20, transcendentals=0),
        name="pack_rows",
    )(leaf_to_panel.reshape(8, 128), potentials)


def place_kernel(me_ref, msg_ref, own_ref, near_ref, far_ref, out_hbm, out, sel, dig, hot_near, sems):
    heads = msg_ref[pl.ds(LINES - 1, DEV, stride=LINES), :]
    turned = jnp.transpose(heads.astype(F32)).astype(I32)
    target = turned[0:CAP] - 1
    high, low = target >> 7, target & 127
    sub = iota((128, 128), 0)
    lane = iota((128, 128), 1)
    for c in range(CAP):
        hot = one_hot(low[c : c + 1] == sub)
        for g in range(4):
            row = jnp.where(high[c : c + 1] == g, 1.0, jnp.where(high[c : c + 1] == g + 4, 256.0, 0.0))
            sel[pl.ds(g * 128, 128), pl.ds(c * 128, 128)] = times_row(hot, row)
        code = heads[:, CAP + c : CAP + c + 1]
        code = jnp.where(lane == 0, code >> 7, jnp.where(lane == 1, code & 127, 0))
        dig[pl.ds(c * 128, 128), pl.ds(2 * BW, 128)] = code.astype(F32).astype(BF16)
    for n in range(TILES):
        for r in range(HALF):
            w = msg_ref[pl.ds(n * HALF + r, DEV, stride=LINES), :]
            for c, hi, lo in ((r, (w >> 16) & 255, w & 255), (r + HALF, (w >> 24) & 255, (w >> 8) & 255)):
                dig[pl.ds(c * 128, 128), pl.ds(n * 256, 128)] = hi.astype(F32).astype(BF16)
                dig[pl.ds(c * 128, 128), pl.ds(n * 256 + 128, 128)] = lo.astype(F32).astype(BF16)
    lane = iota((1, 128), 1)
    own, adjacent, other = (ref[SLOTS : SLOTS + 1, 0:128] for ref in (own_ref, near_ref, far_ref))
    rows = jnp.where(lane < SLOTS, own, jnp.where(lane < 2 * SLOTS, adjacent, other)).astype(I32)
    target = jnp.where((rows < 0) | (lane >= 3 * SLOTS), -1, (rows - me_ref[0] * ROWS) & (TOTAL - 1))
    for g in range(8):
        hot = one_hot(target - g * 128 == sub)
        hot_near[pl.ds(g * 128, 128), 0:128] = hot
        hot_near[pl.ds(g * 128, 128), 128:256] = hot
    near = jnp.concatenate([own_ref[0:SLOTS], near_ref[0:SLOTS], far_ref[0:SLOTS], jnp.zeros((SLOTS, BW), F32)], axis=0)
    first = near.astype(BF16)
    near = jnp.concatenate([first, (near - first.astype(F32)).astype(BF16)], axis=0)
    put = []
    for g in range(2):
        part = sel[pl.ds(g * 256, 256), :]
        codes = mm(part, dig[:, pl.ds(2 * BW, 128)])[:, 0:2].astype(I32)
        scales = []
        for code in (codes & 255, codes >> 8):
            power = jnp.exp2(code[:, 0:1].astype(F32) - 128.0).astype(BF16).astype(F32)
            scales.append(power * (1.0 + code[:, 1:2].astype(F32) * (1.0 / 64.0)))
        spots = [pl.ds(h * 512 + g * 256, 256) for h in range(2)]
        for n in range(TILES):
            cols = pl.ds(n * 128, 128)
            both = mm(part, dig[:, pl.ds(n * 256, 256)]).astype(I32)
            hi, lo = both[:, :128], both[:, 128:]
            values = (((hi & 255) << 8) | (lo & 255), (hi & 0xFF00) | (lo >> 8))
            for h in range(2):
                added = mm(hot_near[spots[h], :], near[:, n * 128 : n * 128 + 128])
                out[spots[h], cols] = (values[h] - 32768).astype(F32) * scales[h] + added
        for h in range(2):
            put.append(pltpu.make_async_copy(out.at[spots[h]], out_hbm.at[spots[h]], sems.at[g * 2 + h]))
            put[-1].start()
    for copy in put:
        copy.wait()


def place(me, arrived, terms):
    return pl.pallas_call(
        place_kernel,
        out_shape=jax.ShapeDtypeStruct((ROWS, BW), F32),
        in_specs=[SMEM] + [VMEM] * 4,
        out_specs=HBM,
        scratch_shapes=[
            pltpu.VMEM((ROWS, BW), F32),
            pltpu.VMEM((ROWS // 2, CAP * 128), BF16),
            pltpu.VMEM((CAP * 128, 2 * BW + 128), BF16),
            pltpu.VMEM((ROWS, 256), BF16),
            pltpu.SemaphoreType.DMA((4,)),
        ],
        compiler_params=pltpu.CompilerParams(vmem_limit_bytes=40 * 2**20),
        cost_estimate=pl.CostEstimate(flops=DEV * CAP * ROWS * 2 * BW, bytes_accessed=4 * 2**20, transcendentals=0),
        name="place_rows",
    )(me, arrived, *terms)


def fetch_kernel(me_ref, own_cols, near_cols, far_cols, density_ref, msg_ref, own_ref, near_ref, far_ref, out_ref):
    base = me_ref[0] * ROWS
    cols = jnp.concatenate([own_cols[...], near_cols[...], far_cols[...], own_cols[...]], axis=1)
    at = ((cols - base) & (TOTAL - 1)).astype(F32)
    at = jnp.transpose(jnp.broadcast_to(at, (128, 128)))[0 : 3 * SLOTS].astype(I32)
    lane = iota((3 * SLOTS, 128), 1)
    hot = jnp.concatenate([one_hot(at - b * 128 == lane) for b in range(8)], axis=1)
    got = mm(hot, density_ref[...]).astype(BF16)
    own_ref[...] = got[0:SLOTS]
    near_ref[...] = got[SLOTS : 2 * SLOTS]
    far_ref[...] = got[2 * SLOTS :]


def fetch(me, cols, density, message):
    rows = jax.ShapeDtypeStruct((SLOTS, BW), BF16)
    return pl.pallas_call(
        fetch_kernel,
        out_shape=(rows, rows, rows, jax.ShapeDtypeStruct(message.shape, message.dtype)),
        in_specs=[SMEM] + [VMEM] * 4 + [HBM],
        out_specs=(VMEM, VMEM, VMEM, HBM),
        input_output_aliases={5: 3},
        compiler_params=pltpu.CompilerParams(vmem_limit_bytes=105 * 2**19),
        cost_estimate=pl.CostEstimate(flops=10**8, bytes_accessed=2**20, transcendentals=0),
        name="fetch_density",
    )(me, *(x.reshape(1, SLOTS) for x in cols), density, message)


STEP = 4


def term_kernel(count_ref, mats_ref, targets_ref, own_ref, far_ref, near_ref, out_ref, acc, vecs):
    step = pl.program_id(0)

    @pl.when(step == 0)
    def _():
        acc[...] = jnp.zeros_like(acc)
        got = own_ref[...].astype(F32) + near_ref[...].astype(F32) + far_ref[...].astype(F32)
        vecs[...] = jnp.concatenate([got, jnp.zeros((128 - SLOTS, BW), F32)], axis=0).astype(BF16)

    lane = iota((BW, 128), 1)
    total = acc[...]
    for k in range(STEP):
        prod = lax.dot_general(mats_ref[k], vecs[...], NT, preferred_element_type=F32)
        total = jnp.where(lane == step * STEP + k, prod, total)
    acc[...] = total

    @pl.when(step == SLOTS // STEP - 1)
    def _():
        live = iota((SLOTS, BW), 0) < count_ref[0]
        out_ref[0:SLOTS, :] = jnp.where(live, jnp.transpose(acc[...])[0:SLOTS], 0.0)
        slot = iota((1, 128), 1) & (SLOTS - 1)
        rows = jnp.where(slot < count_ref[0], targets_ref[...], -1).astype(F32)
        for n in range(TILES):
            out_ref[SLOTS : SLOTS + 8, n * 128 : n * 128 + 128] = jnp.broadcast_to(rows, (8, 128))


def make_terms(count, mats, targets, rows):
    def whole(rows, width):
        return pl.BlockSpec((rows, width), lambda i: (0, 0))

    return pl.pallas_call(
        term_kernel,
        grid=(SLOTS // STEP,),
        out_shape=jax.ShapeDtypeStruct((SLOTS + 8, BW), F32),
        in_specs=[SMEM, pl.BlockSpec((STEP, BW, BW), lambda i: (i, 0, 0)), whole(1, 128)] + [whole(SLOTS, BW)] * 3,
        out_specs=whole(SLOTS + 8, BW),
        scratch_shapes=[pltpu.VMEM((BW, 128), F32), pltpu.VMEM((128, BW), BF16)],
        compiler_params=pltpu.CompilerParams(vmem_limit_bytes=20 * 2**20),
        cost_estimate=pl.CostEstimate(flops=6 * 10**10, bytes_accessed=SLOTS * BW * BW * 2, transcendentals=0),
        name="near_terms",
    )(count, mats, targets, *rows)


def swap_near(value):
    return lax.ppermute(value, AXES, [(i, i ^ 1) for i in range(DEV)])


def swap_far(value):
    return lax.ppermute(value, AXES, [(i, (i - 1 + 2 * (i % 2)) % DEV) for i in range(DEV)])


def on_device(potentials, leaf_to_panel, density, corrections, correction_rows, correction_cols, block_count):
    me = lax.axis_index(AXES).astype(I32).reshape(1)
    cols = (correction_cols, swap_near(correction_cols), swap_far(correction_cols))
    message = pack(leaf_to_panel, potentials)
    own, for_near, for_far, message = fetch(me, cols, density, message)
    rows = (own, swap_far(for_far), swap_near(for_near))
    arrived = lax.all_to_all(
        message.reshape(DEV, LINES, 1, 128), AXES, split_axis=0, concat_axis=0, tiled=True
    ).reshape(DEV * LINES, 128)
    targets = jnp.tile(correction_rows, 128 // SLOTS).reshape(1, 128)
    term = make_terms(block_count, corrections, targets, rows)
    terms = (term, swap_near(term), swap_far(term))
    return place(me, arrived, terms)


def solution(mesh):
    rows = P(AXES, None)
    flat = P(AXES)
    return jax.shard_map(
        on_device,
        mesh=mesh,
        in_specs=(rows, flat, rows, P(AXES, None, None), flat, flat, flat),
        out_specs=rows,
        check_vma=False,
    )
```

```python
import functools

import jax
import jax.numpy as jnp
from jax import lax
from jax.experimental import pallas as pl
from jax.experimental.pallas import tpu as pltpu
from jax.sharding import PartitionSpec as P

AXES = ("leaf", "panel")
DEV = 128
CAP = 16
HALF = CAP // 2
ROWS = 1024
BW = 384
TILES = BW // 128
LINES = HALF * TILES + 1
SLOTS = 32
TOTAL = DEV * ROWS
F32, BF16, I32 = jnp.float32, jnp.bfloat16, jnp.int32
NT = (((1,), (1,)), ((), ()))
VMEM = pl.BlockSpec(memory_space=pltpu.VMEM)
SMEM = pl.BlockSpec(memory_space=pltpu.SMEM)
HBM = pl.BlockSpec(memory_space=pltpu.HBM)


def iota(shape, dim):
    return lax.broadcasted_iota(I32, shape, dim)


def one_hot(mask):
    return jnp.where(mask, 1.0, 0.0).astype(BF16)


def row16(row):
    return jnp.broadcast_to(row, (16, 128)).astype(BF16)[None]


def times_row(block, row):
    return (block.reshape(8, 16, 128) * row16(row)).reshape(128, 128)


def mm(a, b):
    return jnp.dot(a, b, preferred_element_type=F32)


def pack_kernel(map_hbm, pot_hbm, out_hbm, place, pot, msg, sel, dig, head, sems):
    get_map = pltpu.make_async_copy(map_hbm, place, sems.at[0])
    get_map.start()
    get_pot = []
    for g in range(4):
        rows = pl.ds(g * 256, 256)
        get_pot.append(pltpu.make_async_copy(pot_hbm.at[rows], pot.at[rows], sems.at[1 + g]))
        get_pot[g].start()
    get_map.wait()

    dest, label = place[...] >> 10, (place[...] & (ROWS - 1)) + 1
    sub = iota((128, 128), 0)
    before = jnp.concatenate([one_hot(sub < iota((128, 128), 1)), one_hot(sub >= 0)], axis=1)
    hits = [dest[b : b + 1, :] == sub for b in range(8)]
    hot = [one_hot(h) for h in hits]
    counts = mm(jnp.concatenate(hot, axis=0), before)
    carry = jnp.zeros((128, 128), F32)
    ranks = []
    for b in range(8):
        part = counts[b * 128 : b * 128 + 128]
        ranks.append(jnp.sum(jnp.where(hits[b], part[:, :128] + carry, 0.0), axis=0, keepdims=True))
        carry = carry + part[:, 128:]
    low = sub & (CAP - 1)
    ranked = []
    for b in range(8):
        lanes = pl.ds(b * 128, 128)
        for r in range(HALF):
            weight = jnp.where(ranks[b] == r, 1.0, jnp.where(ranks[b] == r + HALF, 256.0, 0.0))
            block = times_row(hot[b], weight)
            for g in range(4):
                sel[pl.ds(g * 256 + r * 32, 32), lanes] = block[g * 32 : g * 32 + 32]
        ranked.append(one_hot(ranks[b].astype(I32) == low))

    for g in range(8):
        if g % 2 == 0:
            get_pot[g // 2].wait()
        rows = pl.ds(g * 128, 128)
        x = pot[rows, :]
        top = jnp.max(jnp.abs(x), axis=1, keepdims=True)
        step = jnp.maximum(top * (1.0 / 32766.0), 2.0**-100)
        expo = jnp.floor(jnp.log2(step) + 1e-3)
        power = jnp.exp2(expo).astype(BF16).astype(F32)
        mant = jnp.maximum(jnp.ceil((step / power - 1.0) * 64.0), 0.0)
        scale = power * (1.0 + mant * (1.0 / 64.0))
        q = jnp.clip(jnp.round(x * (1.0 / scale)), -32767.0, 32767.0)
        hi = jnp.floor(q * (1.0 / 256.0))
        lo = q - hi * 256.0
        hi = hi + 128.0
        for n in range(TILES):
            dig[rows, pl.ds(n * 256, 128)] = hi[:, n * 128 : n * 128 + 128].astype(BF16)
            dig[rows, pl.ds(n * 256 + 128, 128)] = lo[:, n * 128 : n * 128 + 128].astype(BF16)
        lane = iota((128, 128), 1)
        head[rows, :] = jnp.where(lane == 0, expo + 128.0, jnp.where(lane == 1, mant, 0.0)).astype(BF16)
    eye = one_hot(iota((16, 128), 0) == iota((16, 128), 1))
    codes = lax.dot_general(eye, head[...], NT, preferred_element_type=F32)

    digits = [[], [], [], []]
    for b in range(8):
        lab = label[b : b + 1, :]
        cols = slice(b * 128, b * 128 + 128)
        for k, row in enumerate(
            ((lab >> 7).astype(F32), (lab & 127).astype(F32), codes[0:1, cols], codes[1:2, cols])
        ):
            digits[k].append(times_row(hot[b], row))
    left = jnp.concatenate([jnp.concatenate(d, axis=1) for d in digits], axis=0)
    meta = lax.dot_general(left, jnp.concatenate(ranked, axis=1), NT, preferred_element_type=F32).astype(I32)
    words = jnp.where(
        iota((128, 128), 1) < CAP, meta[0:128] * 128 + meta[128:256], meta[256:384] * 128 + meta[384:512]
    )
    msg[pl.ds(LINES - 1, DEV, stride=LINES), :] = words

    put = []
    for g in range(4):
        for n in range(TILES):
            both = mm(sel[pl.ds(g * 256, 256), :], dig[:, pl.ds(n * 256, 256)]).astype(I32)
            w = (both[:, :128] << 16) | both[:, 128:]
            for r in range(HALF):
                msg[pl.ds(g * 32 * LINES + n * HALF + r, 32, stride=LINES), :] = w[r * 32 : r * 32 + 32]
        lines = pl.ds(g * 32 * LINES, 32 * LINES)
        put.append(pltpu.make_async_copy(msg.at[lines], out_hbm.at[lines], sems.at[5 + g]))
        put[g].start()
    for copy in put:
        copy.wait()


def pack(leaf_to_panel, potentials):
    return pl.pallas_call(
        pack_kernel,
        out_shape=jax.ShapeDtypeStruct((DEV * LINES, 128), I32),
        in_specs=[HBM, HBM],
        out_specs=HBM,
        scratch_shapes=[
            pltpu.VMEM((8, 128), I32),
            pltpu.VMEM((ROWS, BW), F32),
            pltpu.VMEM((DEV * LINES, 128), I32),
            pltpu.VMEM((DEV * HALF, ROWS), BF16),
            pltpu.VMEM((ROWS, 2 * BW), BF16),
            pltpu.VMEM((ROWS, 128), BF16),
            pltpu.SemaphoreType.DMA((9,)),
        ],
        compiler_params=pltpu.CompilerParams(vmem_limit_bytes=60 * 2**20),
        cost_estimate=pl.CostEstimate(flops=2 * DEV * CAP * ROWS * 2 * BW, bytes_accessed=4 * 2**20, transcendentals=0),
        name="pack_rows",
    )(leaf_to_panel.reshape(8, 128), potentials)


def place_kernel(me_ref, msg_ref, own_ref, near_ref, far_ref, out_hbm, out, sel, dig, hot_near, sems):
    heads = msg_ref[pl.ds(LINES - 1, DEV, stride=LINES), :]
    turned = jnp.transpose(heads.astype(F32)).astype(I32)
    target = turned[0:CAP] - 1
    high, low = target >> 7, target & 127
    sub = iota((128, 128), 0)
    lane = iota((128, 128), 1)
    for c in range(CAP):
        hot = one_hot(low[c : c + 1] == sub)
        for g in range(4):
            row = jnp.where(high[c : c + 1] == g, 1.0, jnp.where(high[c : c + 1] == g + 4, 256.0, 0.0))
            sel[pl.ds(g * 128, 128), pl.ds(c * 128, 128)] = times_row(hot, row)
        code = heads[:, CAP + c : CAP + c + 1]
        code = jnp.where(lane == 0, code >> 7, jnp.where(lane == 1, code & 127, 0))
        dig[pl.ds(c * 128, 128), pl.ds(2 * BW, 128)] = code.astype(F32).astype(BF16)
    for n in range(TILES):
        for r in range(HALF):
            w = msg_ref[pl.ds(n * HALF + r, DEV, stride=LINES), :]
            for c, hi, lo in ((r, (w >> 16) & 255, w & 255), (r + HALF, (w >> 24) & 255, (w >> 8) & 255)):
                dig[pl.ds(c * 128, 128), pl.ds(n * 256, 128)] = hi.astype(F32).astype(BF16)
                dig[pl.ds(c * 128, 128), pl.ds(n * 256 + 128, 128)] = lo.astype(F32).astype(BF16)
    lane = iota((1, 128), 1)
    own, adjacent, other = (ref[SLOTS : SLOTS + 1, 0:128] for ref in (own_ref, near_ref, far_ref))
    rows = jnp.where(lane < SLOTS, own, jnp.where(lane < 2 * SLOTS, adjacent, other)).astype(I32)
    target = jnp.where((rows < 0) | (lane >= 3 * SLOTS), -1, (rows - me_ref[0] * ROWS) & (TOTAL - 1))
    for g in range(8):
        hot = one_hot(target - g * 128 == sub)
        hot_near[pl.ds(g * 128, 128), 0:128] = hot
        hot_near[pl.ds(g * 128, 128), 128:256] = hot
    near = jnp.concatenate([own_ref[0:SLOTS], near_ref[0:SLOTS], far_ref[0:SLOTS], jnp.zeros((SLOTS, BW), F32)], axis=0)
    first = near.astype(BF16)
    near = jnp.concatenate([first, (near - first.astype(F32)).astype(BF16)], axis=0)
    put = []
    for g in range(2):
        part = sel[pl.ds(g * 256, 256), :]
        codes = mm(part, dig[:, pl.ds(2 * BW, 128)])[:, 0:2].astype(I32)
        scales = []
        for code in (codes & 255, codes >> 8):
            power = jnp.exp2(code[:, 0:1].astype(F32) - 128.0).astype(BF16).astype(F32)
            scales.append(power * (1.0 + code[:, 1:2].astype(F32) * (1.0 / 64.0)))
        spots = [pl.ds(h * 512 + g * 256, 256) for h in range(2)]
        for n in range(TILES):
            cols = pl.ds(n * 128, 128)
            both = mm(part, dig[:, pl.ds(n * 256, 256)]).astype(I32)
            hi, lo = both[:, :128], both[:, 128:]
            values = (((hi & 255) << 8) | (lo & 255), (hi & 0xFF00) | (lo >> 8))
            for h in range(2):
                added = mm(hot_near[spots[h], :], near[:, n * 128 : n * 128 + 128])
                out[spots[h], cols] = (values[h] - 32768).astype(F32) * scales[h] + added
        for h in range(2):
            put.append(pltpu.make_async_copy(out.at[spots[h]], out_hbm.at[spots[h]], sems.at[g * 2 + h]))
            put[-1].start()
    for copy in put:
        copy.wait()


def place(me, arrived, terms):
    return pl.pallas_call(
        place_kernel,
        out_shape=jax.ShapeDtypeStruct((ROWS, BW), F32),
        in_specs=[SMEM] + [VMEM] * 4,
        out_specs=HBM,
        scratch_shapes=[
            pltpu.VMEM((ROWS, BW), F32),
            pltpu.VMEM((ROWS // 2, CAP * 128), BF16),
            pltpu.VMEM((CAP * 128, 2 * BW + 128), BF16),
            pltpu.VMEM((ROWS, 256), BF16),
            pltpu.SemaphoreType.DMA((4,)),
        ],
        compiler_params=pltpu.CompilerParams(vmem_limit_bytes=40 * 2**20),
        cost_estimate=pl.CostEstimate(flops=DEV * CAP * ROWS * 2 * BW, bytes_accessed=4 * 2**20, transcendentals=0),
        name="place_rows",
    )(me, arrived, *terms)


def fetch_kernel(me_ref, own_cols, near_cols, far_cols, density_ref, msg_ref, own_ref, near_ref, far_ref, out_ref):
    base = me_ref[0] * ROWS
    cols = jnp.concatenate([own_cols[...], near_cols[...], far_cols[...], own_cols[...]], axis=1)
    at = ((cols - base) & (TOTAL - 1)).astype(F32)
    at = jnp.transpose(jnp.broadcast_to(at, (128, 128)))[0 : 3 * SLOTS].astype(I32)
    lane = iota((3 * SLOTS, 128), 1)
    hot = jnp.concatenate([one_hot(at - b * 128 == lane) for b in range(8)], axis=1)
    got = mm(hot, density_ref[...]).astype(BF16)
    own_ref[...] = got[0:SLOTS]
    near_ref[...] = got[SLOTS : 2 * SLOTS]
    far_ref[...] = got[2 * SLOTS :]


def fetch(me, cols, density, message):
    rows = jax.ShapeDtypeStruct((SLOTS, BW), BF16)
    return pl.pallas_call(
        fetch_kernel,
        out_shape=(rows, rows, rows, jax.ShapeDtypeStruct(message.shape, message.dtype)),
        in_specs=[SMEM] + [VMEM] * 4 + [HBM],
        out_specs=(VMEM, VMEM, VMEM, HBM),
        input_output_aliases={5: 3},
        compiler_params=pltpu.CompilerParams(vmem_limit_bytes=105 * 2**19),
        cost_estimate=pl.CostEstimate(flops=10**8, bytes_accessed=2**20, transcendentals=0),
        name="fetch_density",
    )(me, *(x.reshape(1, SLOTS) for x in cols), density, message)


STEP = 4


def term_kernel(count_ref, mats_ref, targets_ref, own_ref, far_ref, near_ref, out_ref, acc, vecs):
    step = pl.program_id(0)

    @pl.when(step == 0)
    def _():
        acc[...] = jnp.zeros_like(acc)
        got = own_ref[...].astype(F32) + near_ref[...].astype(F32) + far_ref[...].astype(F32)
        vecs[...] = jnp.concatenate([got, jnp.zeros((128 - SLOTS, BW), F32)], axis=0).astype(BF16)

    lane = iota((BW, 128), 1)
    total = acc[...]
    for k in range(STEP):
        prod = lax.dot_general(mats_ref[k], vecs[...], NT, preferred_element_type=F32)
        total = jnp.where(lane == step * STEP + k, prod, total)
    acc[...] = total

    @pl.when(step == SLOTS // STEP - 1)
    def _():
        live = iota((SLOTS, BW), 0) < count_ref[0]
        out_ref[0:SLOTS, :] = jnp.where(live, jnp.transpose(acc[...])[0:SLOTS], 0.0)
        slot = iota((1, 128), 1) & (SLOTS - 1)
        rows = jnp.where(slot < count_ref[0], targets_ref[...], -1).astype(F32)
        for n in range(TILES):
            out_ref[SLOTS : SLOTS + 8, n * 128 : n * 128 + 128] = jnp.broadcast_to(rows, (8, 128))


def make_terms(count, mats, targets, rows):
    def whole(rows, width):
        return pl.BlockSpec((rows, width), lambda i: (0, 0))

    return pl.pallas_call(
        term_kernel,
        grid=(SLOTS // STEP,),
        out_shape=jax.ShapeDtypeStruct((SLOTS + 8, BW), F32),
        in_specs=[SMEM, pl.BlockSpec((STEP, BW, BW), lambda i: (i, 0, 0)), whole(1, 128)] + [whole(SLOTS, BW)] * 3,
        out_specs=whole(SLOTS + 8, BW),
        scratch_shapes=[pltpu.VMEM((BW, 128), F32), pltpu.VMEM((128, BW), BF16)],
        compiler_params=pltpu.CompilerParams(vmem_limit_bytes=46 * 2**20),
        cost_estimate=pl.CostEstimate(flops=6 * 10**10, bytes_accessed=SLOTS * BW * BW * 2, transcendentals=0),
        name="near_terms",
    )(count, mats, targets, *rows)


def swap_near(value):
    return lax.ppermute(value, AXES, [(i, i ^ 1) for i in range(DEV)])


def swap_far(value):
    return lax.ppermute(value, AXES, [(i, (i - 1 + 2 * (i % 2)) % DEV) for i in range(DEV)])


def on_device(potentials, leaf_to_panel, density, corrections, correction_rows, correction_cols, block_count):
    me = lax.axis_index(AXES).astype(I32).reshape(1)
    cols = (correction_cols, swap_near(correction_cols), swap_far(correction_cols))
    message = pack(leaf_to_panel, potentials)
    own, for_near, for_far, message = fetch(me, cols, density, message)
    rows = (own, swap_far(for_far), swap_near(for_near))
    arrived = lax.all_to_all(
        message.reshape(DEV, LINES, 1, 128), AXES, split_axis=0, concat_axis=0, tiled=True
    ).reshape(DEV * LINES, 128)
    targets = jnp.tile(correction_rows, 128 // SLOTS).reshape(1, 128)
    term = make_terms(block_count, corrections, targets, rows)
    terms = (term, swap_near(term), swap_far(term))
    return place(me, arrived, terms)


def solution(mesh):
    rows = P(AXES, None)
    flat = P(AXES)
    return jax.shard_map(
        on_device,
        mesh=mesh,
        in_specs=(rows, flat, rows, P(AXES, None, None), flat, flat, flat),
        out_specs=rows,
        check_vma=False,
    )
```

```python
import functools

import jax
import jax.numpy as jnp
from jax import lax
from jax.experimental import pallas as pl
from jax.experimental.pallas import tpu as pltpu
from jax.sharding import PartitionSpec as P

AXES = ("leaf", "panel")
DEV = 128
CAP = 16
HALF = CAP // 2
ROWS = 1024
BW = 384
TILES = BW // 128
LINES = HALF * TILES + 1
SLOTS = 32
TOTAL = DEV * ROWS
F32, BF16, I32 = jnp.float32, jnp.bfloat16, jnp.int32
NT = (((1,), (1,)), ((), ()))
VMEM = pl.BlockSpec(memory_space=pltpu.VMEM)
SMEM = pl.BlockSpec(memory_space=pltpu.SMEM)
HBM = pl.BlockSpec(memory_space=pltpu.HBM)


def iota(shape, dim):
    return lax.broadcasted_iota(I32, shape, dim)


def one_hot(mask):
    return jnp.where(mask, 1.0, 0.0).astype(BF16)


def row16(row):
    return jnp.broadcast_to(row, (16, 128)).astype(BF16)[None]


def times_row(block, row):
    return (block.reshape(8, 16, 128) * row16(row)).reshape(128, 128)


def mm(a, b):
    return jnp.dot(a, b, preferred_element_type=F32)


def pack_kernel(map_hbm, pot_hbm, out_hbm, place, pot, msg, sel, dig, head, sems):
    get_map = pltpu.make_async_copy(map_hbm, place, sems.at[0])
    get_map.start()
    get_pot = []
    for g in range(4):
        rows = pl.ds(g * 256, 256)
        get_pot.append(pltpu.make_async_copy(pot_hbm.at[rows], pot.at[rows], sems.at[1 + g]))
        get_pot[g].start()
    get_map.wait()

    dest, label = place[...] >> 10, (place[...] & (ROWS - 1)) + 1
    sub = iota((128, 128), 0)
    before = jnp.concatenate([one_hot(sub < iota((128, 128), 1)), one_hot(sub >= 0)], axis=1)
    hits = [dest[b : b + 1, :] == sub for b in range(8)]
    hot = [one_hot(h) for h in hits]
    counts = mm(jnp.concatenate(hot, axis=0), before)
    carry = jnp.zeros((128, 128), F32)
    ranks = []
    for b in range(8):
        part = counts[b * 128 : b * 128 + 128]
        ranks.append(jnp.sum(jnp.where(hits[b], part[:, :128] + carry, 0.0), axis=0, keepdims=True))
        carry = carry + part[:, 128:]
    low = sub & (CAP - 1)
    ranked = []
    for b in range(8):
        lanes = pl.ds(b * 128, 128)
        for r in range(HALF):
            weight = jnp.where(ranks[b] == r, 1.0, jnp.where(ranks[b] == r + HALF, 256.0, 0.0))
            block = times_row(hot[b], weight)
            for g in range(4):
                sel[pl.ds(g * 256 + r * 32, 32), lanes] = block[g * 32 : g * 32 + 32]
        ranked.append(one_hot(ranks[b].astype(I32) == low))

    for g in range(8):
        if g % 2 == 0:
            get_pot[g // 2].wait()
        rows = pl.ds(g * 128, 128)
        x = pot[rows, :]
        top = jnp.max(jnp.abs(x), axis=1, keepdims=True)
        step = jnp.maximum(top * (1.0 / 32766.0), 2.0**-100)
        expo = jnp.floor(jnp.log2(step) + 1e-3)
        power = jnp.exp2(expo).astype(BF16).astype(F32)
        mant = jnp.maximum(jnp.ceil((step / power - 1.0) * 64.0), 0.0)
        scale = power * (1.0 + mant * (1.0 / 64.0))
        q = jnp.clip(jnp.round(x * (1.0 / scale)), -32767.0, 32767.0)
        hi = jnp.floor(q * (1.0 / 256.0))
        lo = q - hi * 256.0
        hi = hi + 128.0
        for n in range(TILES):
            dig[rows, pl.ds(n * 256, 128)] = hi[:, n * 128 : n * 128 + 128].astype(BF16)
            dig[rows, pl.ds(n * 256 + 128, 128)] = lo[:, n * 128 : n * 128 + 128].astype(BF16)
        lane = iota((128, 128), 1)
        head[rows, :] = jnp.where(lane == 0, expo + 128.0, jnp.where(lane == 1, mant, 0.0)).astype(BF16)
    eye = one_hot(iota((16, 128), 0) == iota((16, 128), 1))
    codes = lax.dot_general(eye, head[...], NT, preferred_element_type=F32)

    digits = [[], [], [], []]
    for b in range(8):
        lab = label[b : b + 1, :]
        cols = slice(b * 128, b * 128 + 128)
        for k, row in enumerate(
            ((lab >> 7).astype(F32), (lab & 127).astype(F32), codes[0:1, cols], codes[1:2, cols])
        ):
            digits[k].append(times_row(hot[b], row))
    left = jnp.concatenate([jnp.concatenate(d, axis=1) for d in digits], axis=0)
    meta = lax.dot_general(left, jnp.concatenate(ranked, axis=1), NT, preferred_element_type=F32).astype(I32)
    words = jnp.where(
        iota((128, 128), 1) < CAP, meta[0:128] * 128 + meta[128:256], meta[256:384] * 128 + meta[384:512]
    )
    msg[pl.ds(LINES - 1, DEV, stride=LINES), :] = words

    put = []
    for g in range(4):
        for n in range(TILES):
            both = mm(sel[pl.ds(g * 256, 256), :], dig[:, pl.ds(n * 256, 256)]).astype(I32)
            w = (both[:, :128] << 16) | both[:, 128:]
            for r in range(HALF):
                msg[pl.ds(g * 32 * LINES + n * HALF + r, 32, stride=LINES), :] = w[r * 32 : r * 32 + 32]
        lines = pl.ds(g * 32 * LINES, 32 * LINES)
        put.append(pltpu.make_async_copy(msg.at[lines], out_hbm.at[lines], sems.at[5 + g]))
        put[g].start()
    for copy in put:
        copy.wait()


def pack(leaf_to_panel, potentials):
    return pl.pallas_call(
        pack_kernel,
        out_shape=jax.ShapeDtypeStruct((DEV * LINES, 128), I32),
        in_specs=[HBM, HBM],
        out_specs=HBM,
        scratch_shapes=[
            pltpu.VMEM((8, 128), I32),
            pltpu.VMEM((ROWS, BW), F32),
            pltpu.VMEM((DEV * LINES, 128), I32),
            pltpu.VMEM((DEV * HALF, ROWS), BF16),
            pltpu.VMEM((ROWS, 2 * BW), BF16),
            pltpu.VMEM((ROWS, 128), BF16),
            pltpu.SemaphoreType.DMA((9,)),
        ],
        compiler_params=pltpu.CompilerParams(vmem_limit_bytes=60 * 2**20),
        cost_estimate=pl.CostEstimate(flops=2 * DEV * CAP * ROWS * 2 * BW, bytes_accessed=4 * 2**20, transcendentals=0),
        name="pack_rows",
    )(leaf_to_panel.reshape(8, 128), potentials)


def place_kernel(me_ref, msg_ref, own_ref, near_ref, far_ref, out_hbm, out, sel, dig, hot_near, sems):
    heads = msg_ref[pl.ds(LINES - 1, DEV, stride=LINES), :]
    turned = jnp.transpose(heads.astype(F32)).astype(I32)
    target = turned[0:CAP] - 1
    high, low = target >> 7, target & 127
    sub = iota((128, 128), 0)
    lane = iota((128, 128), 1)
    for c in range(CAP):
        hot = one_hot(low[c : c + 1] == sub)
        for g in range(4):
            row = jnp.where(high[c : c + 1] == g, 1.0, jnp.where(high[c : c + 1] == g + 4, 256.0, 0.0))
            sel[pl.ds(g * 128, 128), pl.ds(c * 128, 128)] = times_row(hot, row)
        code = heads[:, CAP + c : CAP + c + 1]
        code = jnp.where(lane == 0, code >> 7, jnp.where(lane == 1, code & 127, 0))
        dig[pl.ds(c * 128, 128), pl.ds(2 * BW, 128)] = code.astype(F32).astype(BF16)
    for n in range(TILES):
        for r in range(HALF):
            w = msg_ref[pl.ds(n * HALF + r, DEV, stride=LINES), :]
            for c, hi, lo in ((r, (w >> 16) & 255, w & 255), (r + HALF, (w >> 24) & 255, (w >> 8) & 255)):
                dig[pl.ds(c * 128, 128), pl.ds(n * 256, 128)] = hi.astype(F32).astype(BF16)
                dig[pl.ds(c * 128, 128), pl.ds(n * 256 + 128, 128)] = lo.astype(F32).astype(BF16)
    lane = iota((1, 128), 1)
    own, adjacent, other = (ref[SLOTS : SLOTS + 1, 0:128] for ref in (own_ref, near_ref, far_ref))
    rows = jnp.where(lane < SLOTS, own, jnp.where(lane < 2 * SLOTS, adjacent, other)).astype(I32)
    target = jnp.where((rows < 0) | (lane >= 3 * SLOTS), -1, (rows - me_ref[0] * ROWS) & (TOTAL - 1))
    for g in range(8):
        hot = one_hot(target - g * 128 == sub)
        hot_near[pl.ds(g * 128, 128), 0:128] = hot
        hot_near[pl.ds(g * 128, 128), 128:256] = hot
    near = jnp.concatenate([own_ref[0:SLOTS], near_ref[0:SLOTS], far_ref[0:SLOTS], jnp.zeros((SLOTS, BW), F32)], axis=0)
    first = near.astype(BF16)
    near = jnp.concatenate([first, (near - first.astype(F32)).astype(BF16)], axis=0)
    put = []
    for g in range(2):
        part = sel[pl.ds(g * 256, 256), :]
        codes = mm(part, dig[:, pl.ds(2 * BW, 128)])[:, 0:2].astype(I32)
        scales = []
        for code in (codes & 255, codes >> 8):
            power = jnp.exp2(code[:, 0:1].astype(F32) - 128.0).astype(BF16).astype(F32)
            scales.append(power * (1.0 + code[:, 1:2].astype(F32) * (1.0 / 64.0)))
        spots = [pl.ds(h * 512 + g * 256, 256) for h in range(2)]
        for n in range(TILES):
            cols = pl.ds(n * 128, 128)
            both = mm(part, dig[:, pl.ds(n * 256, 256)]).astype(I32)
            hi, lo = both[:, :128], both[:, 128:]
            values = (((hi & 255) << 8) | (lo & 255), (hi & 0xFF00) | (lo >> 8))
            for h in range(2):
                added = mm(hot_near[spots[h], :], near[:, n * 128 : n * 128 + 128])
                out[spots[h], cols] = (values[h] - 32768).astype(F32) * scales[h] + added
        for h in range(2):
            put.append(pltpu.make_async_copy(out.at[spots[h]], out_hbm.at[spots[h]], sems.at[g * 2 + h]))
            put[-1].start()
    for copy in put:
        copy.wait()


def place(me, arrived, terms):
    return pl.pallas_call(
        place_kernel,
        out_shape=jax.ShapeDtypeStruct((ROWS, BW), F32),
        in_specs=[SMEM] + [VMEM] * 4,
        out_specs=HBM,
        scratch_shapes=[
            pltpu.VMEM((ROWS, BW), F32),
            pltpu.VMEM((ROWS // 2, CAP * 128), BF16),
            pltpu.VMEM((CAP * 128, 2 * BW + 128), BF16),
            pltpu.VMEM((ROWS, 256), BF16),
            pltpu.SemaphoreType.DMA((4,)),
        ],
        compiler_params=pltpu.CompilerParams(vmem_limit_bytes=40 * 2**20),
        cost_estimate=pl.CostEstimate(flops=DEV * CAP * ROWS * 2 * BW, bytes_accessed=4 * 2**20, transcendentals=0),
        name="place_rows",
    )(me, arrived, *terms)


def fetch_kernel(me_ref, own_cols, near_cols, far_cols, density_ref, msg_ref, own_ref, near_ref, far_ref, out_ref):
    base = me_ref[0] * ROWS
    cols = jnp.concatenate([own_cols[...], near_cols[...], far_cols[...], own_cols[...]], axis=1)
    at = ((cols - base) & (TOTAL - 1)).astype(F32)
    at = jnp.transpose(jnp.broadcast_to(at, (128, 128)))[0 : 3 * SLOTS].astype(I32)
    lane = iota((3 * SLOTS, 128), 1)
    hot = jnp.concatenate([one_hot(at - b * 128 == lane) for b in range(8)], axis=1)
    got = mm(hot, density_ref[...]).astype(BF16)
    own_ref[...] = got[0:SLOTS]
    near_ref[...] = got[SLOTS : 2 * SLOTS]
    far_ref[...] = got[2 * SLOTS :]


def fetch(me, cols, density, message):
    rows = jax.ShapeDtypeStruct((SLOTS, BW), BF16)
    return pl.pallas_call(
        fetch_kernel,
        out_shape=(rows, rows, rows, jax.ShapeDtypeStruct(message.shape, message.dtype)),
        in_specs=[SMEM] + [VMEM] * 4 + [HBM],
        out_specs=(VMEM, VMEM, VMEM, HBM),
        input_output_aliases={5: 3},
        compiler_params=pltpu.CompilerParams(vmem_limit_bytes=105 * 2**19),
        cost_estimate=pl.CostEstimate(flops=10**8, bytes_accessed=2**20, transcendentals=0),
        name="fetch_density",
    )(me, *(x.reshape(1, SLOTS) for x in cols), density, message)


STEP = 4


def term_kernel(me_ref, count_ref, mats_ref, sources_ref, targets_ref, own_ref, far_ref, near_ref, block_ref, out_ref, acc, vecs):
    step = pl.program_id(0)

    @pl.when(step == 0)
    def _():
        acc[...] = jnp.zeros_like(acc)
        got = own_ref[...].astype(F32) + near_ref[...].astype(F32) + far_ref[...].astype(F32)
        other = (me_ref[0] - 1 + 2 * (me_ref[0] & 1)) & (DEV - 1)
        at = ((sources_ref[...] - other * ROWS) & (TOTAL - 1)).astype(F32)
        at = jnp.transpose(jnp.broadcast_to(at, (128, 128)))[0:SLOTS].astype(I32)
        spot = iota((SLOTS, 128), 1)
        hot = jnp.concatenate([one_hot(at - b * 128 == spot) for b in range(8)], axis=1)
        got = got + mm(hot, block_ref[...])
        vecs[...] = jnp.concatenate([got, jnp.zeros((128 - SLOTS, BW), F32)], axis=0).astype(BF16)

    lane = iota((BW, 128), 1)
    total = acc[...]
    for k in range(STEP):
        prod = lax.dot_general(mats_ref[k], vecs[...], NT, preferred_element_type=F32)
        total = jnp.where(lane == step * STEP + k, prod, total)
    acc[...] = total

    @pl.when(step == SLOTS // STEP - 1)
    def _():
        live = iota((SLOTS, BW), 0) < count_ref[0]
        out_ref[0:SLOTS, :] = jnp.where(live, jnp.transpose(acc[...])[0:SLOTS], 0.0)
        slot = iota((1, 128), 1) & (SLOTS - 1)
        rows = jnp.where(slot < count_ref[0], targets_ref[...], -1).astype(F32)
        for n in range(TILES):
            out_ref[SLOTS : SLOTS + 8, n * 128 : n * 128 + 128] = jnp.broadcast_to(rows, (8, 128))


def make_terms(me, count, mats, sources, targets, rows, block):
    def whole(rows, width):
        return pl.BlockSpec((rows, width), lambda i: (0, 0))

    return pl.pallas_call(
        term_kernel,
        grid=(SLOTS // STEP,),
        out_shape=jax.ShapeDtypeStruct((SLOTS + 8, BW), F32),
        in_specs=[SMEM, SMEM, pl.BlockSpec((STEP, BW, BW), lambda i: (i, 0, 0))]
        + [whole(1, 128)] * 2
        + [whole(SLOTS, BW)] * 3
        + [whole(ROWS, BW)],
        out_specs=whole(SLOTS + 8, BW),
        scratch_shapes=[pltpu.VMEM((BW, 128), F32), pltpu.VMEM((128, BW), BF16)],
        compiler_params=pltpu.CompilerParams(vmem_limit_bytes=20 * 2**20),
        cost_estimate=pl.CostEstimate(flops=6 * 10**10, bytes_accessed=SLOTS * BW * BW * 2, transcendentals=0),
        name="near_terms",
    )(me, count, mats, sources, targets, *rows, block)


def swap_near(value):
    return lax.ppermute(value, AXES, [(i, i ^ 1) for i in range(DEV)])


FAR = [(i, (i - 1 + 2 * (i % 2)) % DEV) for i in range(DEV)]


def swap_far(value):
    return lax.ppermute(value, AXES, FAR)


def swap_inner(value):
    size = lax.axis_size("panel")
    return lax.ppermute(value, AXES, [(i, j) for i, j in FAR if i // size == j // size])


def swap_cross(value):
    size = lax.axis_size("panel")
    return lax.ppermute(value, AXES, [(i, j) for i, j in FAR if i // size != j // size])


def on_device(potentials, leaf_to_panel, density, corrections, correction_rows, correction_cols, block_count):
    me = lax.axis_index(AXES).astype(I32).reshape(1)
    block = swap_cross(density)
    cols = (correction_cols, swap_near(correction_cols), swap_inner(correction_cols))
    message = pack(leaf_to_panel, potentials)
    own, for_near, for_far, message = fetch(me, cols, density, message)
    rows = (own, swap_inner(for_far), swap_near(for_near))
    arrived = lax.all_to_all(
        message.reshape(DEV, LINES, 1, 128), AXES, split_axis=0, concat_axis=0, tiled=True
    ).reshape(DEV * LINES, 128)
    sources, targets = (jnp.tile(x, 128 // SLOTS).reshape(1, 128) for x in (correction_cols, correction_rows))
    term = make_terms(me, block_count, corrections, sources, targets, rows, block)
    terms = (term, swap_far(term), swap_near(term))
    return place(me, arrived, terms)


def solution(mesh):
    rows = P(AXES, None)
    flat = P(AXES)
    return jax.shard_map(
        on_device,
        mesh=mesh,
        in_specs=(rows, flat, rows, P(AXES, None, None), flat, flat, flat),
        out_specs=rows,
        check_vma=False,
    )
```

```python
import functools

import jax
import jax.numpy as jnp
from jax import lax
from jax.experimental import pallas as pl
from jax.experimental.pallas import tpu as pltpu
from jax.sharding import PartitionSpec as P

AXES = ("leaf", "panel")
DEV = 128
CAP = 16
HALF = CAP // 2
ROWS = 1024
BW = 384
TILES = BW // 128
LINES = HALF * TILES + 1
SLOTS = 32
TOTAL = DEV * ROWS
F32, BF16, I32 = jnp.float32, jnp.bfloat16, jnp.int32
NT = (((1,), (1,)), ((), ()))
VMEM = pl.BlockSpec(memory_space=pltpu.VMEM)
SMEM = pl.BlockSpec(memory_space=pltpu.SMEM)
HBM = pl.BlockSpec(memory_space=pltpu.HBM)


def iota(shape, dim):
    return lax.broadcasted_iota(I32, shape, dim)


def one_hot(mask):
    return jnp.where(mask, 1.0, 0.0).astype(BF16)


def row16(row):
    return jnp.broadcast_to(row, (16, 128)).astype(BF16)[None]


def times_row(block, row):
    return (block.reshape(8, 16, 128) * row16(row)).reshape(128, 128)


def mm(a, b):
    return jnp.dot(a, b, preferred_element_type=F32)


def pack_kernel(map_hbm, pot_hbm, out_hbm, place, pot, msg, sel, dig, head, sems):
    get_map = pltpu.make_async_copy(map_hbm, place, sems.at[0])
    get_map.start()
    get_pot = []
    for g in range(4):
        rows = pl.ds(g * 256, 256)
        get_pot.append(pltpu.make_async_copy(pot_hbm.at[rows], pot.at[rows], sems.at[1 + g]))
        get_pot[g].start()
    get_map.wait()

    dest, label = place[...] >> 10, (place[...] & (ROWS - 1)) + 1
    sub = iota((128, 128), 0)
    before = jnp.concatenate([one_hot(sub < iota((128, 128), 1)), one_hot(sub >= 0)], axis=1)
    hits = [dest[b : b + 1, :] == sub for b in range(8)]
    hot = [one_hot(h) for h in hits]
    counts = mm(jnp.concatenate(hot, axis=0), before)
    carry = jnp.zeros((128, 128), F32)
    ranks = []
    for b in range(8):
        part = counts[b * 128 : b * 128 + 128]
        ranks.append(jnp.sum(jnp.where(hits[b], part[:, :128] + carry, 0.0), axis=0, keepdims=True))
        carry = carry + part[:, 128:]
    low = sub & (CAP - 1)
    ranked = []
    for b in range(8):
        lanes = pl.ds(b * 128, 128)
        for r in range(HALF):
            weight = jnp.where(ranks[b] == r, 1.0, jnp.where(ranks[b] == r + HALF, 256.0, 0.0))
            block = times_row(hot[b], weight)
            for g in range(4):
                sel[pl.ds(g * 256 + r * 32, 32), lanes] = block[g * 32 : g * 32 + 32]
        ranked.append(one_hot(ranks[b].astype(I32) == low))

    for g in range(8):
        if g % 2 == 0:
            get_pot[g // 2].wait()
        rows = pl.ds(g * 128, 128)
        x = pot[rows, :]
        top = jnp.max(jnp.abs(x), axis=1, keepdims=True)
        step = jnp.maximum(top * (1.0 / 32766.0), 2.0**-100)
        expo = jnp.floor(jnp.log2(step) + 1e-3)
        power = jnp.exp2(expo).astype(BF16).astype(F32)
        mant = jnp.maximum(jnp.ceil((step / power - 1.0) * 64.0), 0.0)
        scale = power * (1.0 + mant * (1.0 / 64.0))
        q = jnp.clip(jnp.round(x * (1.0 / scale)), -32767.0, 32767.0)
        hi = jnp.floor(q * (1.0 / 256.0))
        lo = q - hi * 256.0
        hi = hi + 128.0
        for n in range(TILES):
            dig[rows, pl.ds(n * 256, 128)] = hi[:, n * 128 : n * 128 + 128].astype(BF16)
            dig[rows, pl.ds(n * 256 + 128, 128)] = lo[:, n * 128 : n * 128 + 128].astype(BF16)
        lane = iota((128, 128), 1)
        head[rows, :] = jnp.where(lane == 0, expo + 128.0, jnp.where(lane == 1, mant, 0.0)).astype(BF16)
    eye = one_hot(iota((16, 128), 0) == iota((16, 128), 1))
    codes = lax.dot_general(eye, head[...], NT, preferred_element_type=F32)

    digits = [[], [], [], []]
    for b in range(8):
        lab = label[b : b + 1, :]
        cols = slice(b * 128, b * 128 + 128)
        for k, row in enumerate(
            ((lab >> 7).astype(F32), (lab & 127).astype(F32), codes[0:1, cols], codes[1:2, cols])
        ):
            digits[k].append(times_row(hot[b], row))
    left = jnp.concatenate([jnp.concatenate(d, axis=1) for d in digits], axis=0)
    meta = lax.dot_general(left, jnp.concatenate(ranked, axis=1), NT, preferred_element_type=F32).astype(I32)
    words = jnp.where(
        iota((128, 128), 1) < CAP, meta[0:128] * 128 + meta[128:256], meta[256:384] * 128 + meta[384:512]
    )
    msg[pl.ds(LINES - 1, DEV, stride=LINES), :] = words

    put = []
    for g in range(4):
        for n in range(TILES):
            both = mm(sel[pl.ds(g * 256, 256), :], dig[:, pl.ds(n * 256, 256)]).astype(I32)
            w = (both[:, :128] << 16) | both[:, 128:]
            for r in range(HALF):
                msg[pl.ds(g * 32 * LINES + n * HALF + r, 32, stride=LINES), :] = w[r * 32 : r * 32 + 32]
        lines = pl.ds(g * 32 * LINES, 32 * LINES)
        put.append(pltpu.make_async_copy(msg.at[lines], out_hbm.at[lines], sems.at[5 + g]))
        put[g].start()
    for copy in put:
        copy.wait()


def pack(leaf_to_panel, potentials):
    return pl.pallas_call(
        pack_kernel,
        out_shape=jax.ShapeDtypeStruct((DEV * LINES, 128), I32),
        in_specs=[HBM, HBM],
        out_specs=HBM,
        scratch_shapes=[
            pltpu.VMEM((8, 128), I32),
            pltpu.VMEM((ROWS, BW), F32),
            pltpu.VMEM((DEV * LINES, 128), I32),
            pltpu.VMEM((DEV * HALF, ROWS), BF16),
            pltpu.VMEM((ROWS, 2 * BW), BF16),
            pltpu.VMEM((ROWS, 128), BF16),
            pltpu.SemaphoreType.DMA((9,)),
        ],
        compiler_params=pltpu.CompilerParams(vmem_limit_bytes=60 * 2**20),
        cost_estimate=pl.CostEstimate(flops=2 * DEV * CAP * ROWS * 2 * BW, bytes_accessed=4 * 2**20, transcendentals=0),
        name="pack_rows",
    )(leaf_to_panel.reshape(8, 128), potentials)


def place_kernel(msg_ref, out, sel, dig):
    heads = msg_ref[pl.ds(LINES - 1, DEV, stride=LINES), :]
    turned = jnp.transpose(heads.astype(F32)).astype(I32)
    target = turned[0:CAP] - 1
    high, low = target >> 7, target & 127
    sub = iota((128, 128), 0)
    lane = iota((128, 128), 1)
    for c in range(CAP):
        hot = one_hot(low[c : c + 1] == sub)
        for g in range(4):
            row = jnp.where(high[c : c + 1] == g, 1.0, jnp.where(high[c : c + 1] == g + 4, 256.0, 0.0))
            sel[pl.ds(g * 128, 128), pl.ds(c * 128, 128)] = times_row(hot, row)
        code = heads[:, CAP + c : CAP + c + 1]
        code = jnp.where(lane == 0, code >> 7, jnp.where(lane == 1, code & 127, 0))
        dig[pl.ds(c * 128, 128), pl.ds(2 * BW, 128)] = code.astype(F32).astype(BF16)
    for n in range(TILES):
        for r in range(HALF):
            w = msg_ref[pl.ds(n * HALF + r, DEV, stride=LINES), :]
            for c, hi, lo in ((r, (w >> 16) & 255, w & 255), (r + HALF, (w >> 24) & 255, (w >> 8) & 255)):
                dig[pl.ds(c * 128, 128), pl.ds(n * 256, 128)] = hi.astype(F32).astype(BF16)
                dig[pl.ds(c * 128, 128), pl.ds(n * 256 + 128, 128)] = lo.astype(F32).astype(BF16)
    for g in range(2):
        part = sel[pl.ds(g * 256, 256), :]
        codes = mm(part, dig[:, pl.ds(2 * BW, 128)])[:, 0:2].astype(I32)
        scales = []
        for code in (codes & 255, codes >> 8):
            power = jnp.exp2(code[:, 0:1].astype(F32) - 128.0).astype(BF16).astype(F32)
            scales.append(power * (1.0 + code[:, 1:2].astype(F32) * (1.0 / 64.0)))
        spots = [pl.ds(h * 512 + g * 256, 256) for h in range(2)]
        for n in range(TILES):
            cols = pl.ds(n * 128, 128)
            both = mm(part, dig[:, pl.ds(n * 256, 256)]).astype(I32)
            hi, lo = both[:, :128], both[:, 128:]
            values = (((hi & 255) << 8) | (lo & 255), (hi & 0xFF00) | (lo >> 8))
            for h in range(2):
                out[spots[h], cols] = (values[h] - 32768).astype(F32) * scales[h]


def place(arrived):
    return pl.pallas_call(
        place_kernel,
        out_shape=jax.ShapeDtypeStruct((ROWS, BW), F32),
        in_specs=[VMEM],
        out_specs=VMEM,
        scratch_shapes=[
            pltpu.VMEM((ROWS // 2, CAP * 128), BF16),
            pltpu.VMEM((CAP * 128, 2 * BW + 128), BF16),
        ],
        compiler_params=pltpu.CompilerParams(vmem_limit_bytes=40 * 2**20),
        cost_estimate=pl.CostEstimate(flops=DEV * CAP * ROWS * 2 * BW, bytes_accessed=4 * 2**20, transcendentals=0),
        name="place_rows",
    )(arrived)


def add_kernel(me_ref, placed_ref, own_ref, near_ref, far_ref, out_hbm, out, sems):
    lane = iota((1, 128), 1)
    own, adjacent, other = (ref[SLOTS : SLOTS + 1, 0:128] for ref in (own_ref, near_ref, far_ref))
    rows = jnp.where(lane < SLOTS, own, jnp.where(lane < 2 * SLOTS, adjacent, other)).astype(I32)
    target = jnp.where((rows < 0) | (lane >= 3 * SLOTS), -1, (rows - me_ref[0] * ROWS) & (TOTAL - 1))
    near = jnp.concatenate([own_ref[0:SLOTS], near_ref[0:SLOTS], far_ref[0:SLOTS], jnp.zeros((SLOTS, BW), F32)], axis=0)
    first = near.astype(BF16)
    near = jnp.concatenate([first, (near - first.astype(F32)).astype(BF16)], axis=0)
    sub = iota((256, 128), 0)
    put = []
    for g in range(4):
        hot = one_hot(target - g * 256 == sub)
        spot = pl.ds(g * 256, 256)
        out[spot, :] = placed_ref[spot, :] + mm(jnp.concatenate([hot, hot], axis=1), near)
        put.append(pltpu.make_async_copy(out.at[spot], out_hbm.at[spot], sems.at[g]))
        put[g].start()
    for copy in put:
        copy.wait()


def add_terms(me, placed, terms):
    return pl.pallas_call(
        add_kernel,
        out_shape=jax.ShapeDtypeStruct((ROWS, BW), F32),
        in_specs=[SMEM] + [VMEM] * 4,
        out_specs=HBM,
        scratch_shapes=[pltpu.VMEM((ROWS, BW), F32), pltpu.SemaphoreType.DMA((4,))],
        compiler_params=pltpu.CompilerParams(vmem_limit_bytes=12 * 2**20),
        cost_estimate=pl.CostEstimate(flops=2 * ROWS * 256 * BW, bytes_accessed=4 * 2**20, transcendentals=0),
        name="add_terms",
    )(me, placed, *terms)


def fetch_kernel(me_ref, own_cols, near_cols, far_cols, density_ref, msg_ref, own_ref, near_ref, far_ref, out_ref):
    base = me_ref[0] * ROWS
    cols = jnp.concatenate([own_cols[...], near_cols[...], far_cols[...], own_cols[...]], axis=1)
    at = ((cols - base) & (TOTAL - 1)).astype(F32)
    at = jnp.transpose(jnp.broadcast_to(at, (128, 128)))[0 : 3 * SLOTS].astype(I32)
    lane = iota((3 * SLOTS, 128), 1)
    hot = jnp.concatenate([one_hot(at - b * 128 == lane) for b in range(8)], axis=1)
    got = mm(hot, density_ref[...]).astype(BF16)
    own_ref[...] = got[0:SLOTS]
    near_ref[...] = got[SLOTS : 2 * SLOTS]
    far_ref[...] = got[2 * SLOTS :]


def fetch(me, cols, density, message):
    rows = jax.ShapeDtypeStruct((SLOTS, BW), BF16)
    return pl.pallas_call(
        fetch_kernel,
        out_shape=(rows, rows, rows, jax.ShapeDtypeStruct(message.shape, message.dtype)),
        in_specs=[SMEM] + [VMEM] * 4 + [HBM],
        out_specs=(VMEM, VMEM, VMEM, HBM),
        input_output_aliases={5: 3},
        compiler_params=pltpu.CompilerParams(vmem_limit_bytes=105 * 2**19),
        cost_estimate=pl.CostEstimate(flops=10**8, bytes_accessed=2**20, transcendentals=0),
        name="fetch_density",
    )(me, *(x.reshape(1, SLOTS) for x in cols), density, message)


STEP = 4


def term_kernel(count_ref, mats_ref, targets_ref, own_ref, far_ref, near_ref, out_ref, acc, vecs):
    step = pl.program_id(0)

    @pl.when(step == 0)
    def _():
        acc[...] = jnp.zeros_like(acc)
        got = own_ref[...].astype(F32) + near_ref[...].astype(F32) + far_ref[...].astype(F32)
        vecs[...] = jnp.concatenate([got, jnp.zeros((128 - SLOTS, BW), F32)], axis=0).astype(BF16)

    lane = iota((BW, 128), 1)
    total = acc[...]
    for k in range(STEP):
        prod = lax.dot_general(mats_ref[k], vecs[...], NT, preferred_element_type=F32)
        total = jnp.where(lane == step * STEP + k, prod, total)
    acc[...] = total

    @pl.when(step == SLOTS // STEP - 1)
    def _():
        live = iota((SLOTS, BW), 0) < count_ref[...]
        out_ref[0:SLOTS, :] = jnp.where(live, jnp.transpose(acc[...])[0:SLOTS], 0.0)
        slot = iota((1, 128), 1) & (SLOTS - 1)
        rows = jnp.concatenate([targets_ref[...]] * (128 // SLOTS), axis=1)
        rows = jnp.where(slot < count_ref[...], rows, -1).astype(F32)
        for n in range(TILES):
            out_ref[SLOTS : SLOTS + 8, n * 128 : n * 128 + 128] = jnp.broadcast_to(rows, (8, 128))


def make_terms(count, mats, targets, rows):
    def whole(rows, width):
        return pl.BlockSpec((rows, width), lambda i: (0, 0))

    return pl.pallas_call(
        term_kernel,
        grid=(SLOTS // STEP,),
        out_shape=jax.ShapeDtypeStruct((SLOTS + 8, BW), F32),
        in_specs=[whole(1, 1), pl.BlockSpec((STEP, BW, BW), lambda i: (i, 0, 0)), whole(1, SLOTS)] + [whole(SLOTS, BW)] * 3,
        out_specs=whole(SLOTS + 8, BW),
        scratch_shapes=[pltpu.VMEM((BW, 128), F32), pltpu.VMEM((128, BW), BF16)],
        compiler_params=pltpu.CompilerParams(vmem_limit_bytes=20 * 2**20),
        cost_estimate=pl.CostEstimate(flops=6 * 10**10, bytes_accessed=SLOTS * BW * BW * 2, transcendentals=0),
        name="near_terms",
    )(count, mats, targets, *rows)


def swap_near(value):
    return lax.ppermute(value, AXES, [(i, i ^ 1) for i in range(DEV)])


def swap_far(value):
    return lax.ppermute(value, AXES, [(i, (i - 1 + 2 * (i % 2)) % DEV) for i in range(DEV)])


def on_device(potentials, leaf_to_panel, density, corrections, correction_rows, correction_cols, block_count):
    me = lax.axis_index(AXES).astype(I32).reshape(1)
    cols = (correction_cols, swap_far(correction_cols), swap_near(correction_cols))
    message = pack(leaf_to_panel, potentials)
    own, for_far, for_near, message = fetch(me, cols, density, message)
    rows = (own, swap_far(for_far), swap_near(for_near))
    arrived = lax.all_to_all(
        message.reshape(DEV, LINES, 1, 128), AXES, split_axis=0, concat_axis=0, tiled=True
    ).reshape(DEV * LINES, 128)
    term = make_terms(block_count.reshape(1, 1), corrections, correction_rows.reshape(1, SLOTS), rows)
    terms = (term, swap_far(term), swap_near(term))
    return add_terms(me, place(arrived), terms)


def solution(mesh):
    rows = P(AXES, None)
    flat = P(AXES)
    return jax.shard_map(
        on_device,
        mesh=mesh,
        in_specs=(rows, flat, rows, P(AXES, None, None), flat, flat, flat),
        out_specs=rows,
        check_vma=False,
    )
```

```python
import functools

import jax
import jax.numpy as jnp
from jax import lax
from jax.experimental import pallas as pl
from jax.experimental.pallas import tpu as pltpu
from jax.sharding import PartitionSpec as P

AXES = ("leaf", "panel")
DEV = 128
CAP = 16
HALF = CAP // 2
ROWS = 1024
BW = 384
TILES = BW // 128
LINES = HALF * TILES + 1
SLOTS = 32
TOTAL = DEV * ROWS
F32, BF16, I32 = jnp.float32, jnp.bfloat16, jnp.int32
NT = (((1,), (1,)), ((), ()))
VMEM = pl.BlockSpec(memory_space=pltpu.VMEM)
SMEM = pl.BlockSpec(memory_space=pltpu.SMEM)
HBM = pl.BlockSpec(memory_space=pltpu.HBM)


def iota(shape, dim):
    return lax.broadcasted_iota(I32, shape, dim)


def one_hot(mask):
    return jnp.where(mask, 1.0, 0.0).astype(BF16)


def row16(row):
    return jnp.broadcast_to(row, (16, 128)).astype(BF16)[None]


def times_row(block, row):
    return (block.reshape(8, 16, 128) * row16(row)).reshape(128, 128)


def mm(a, b):
    return jnp.dot(a, b, preferred_element_type=F32)


def pack_kernel(map_hbm, pot_hbm, out_hbm, place, pot, msg, sel, dig, head, half, sems):
    get_map = pltpu.make_async_copy(map_hbm, place, sems.at[0])
    get_map.start()
    get_pot = []
    for g in range(4):
        rows = pl.ds(g * 256, 256)
        get_pot.append(pltpu.make_async_copy(pot_hbm.at[rows], pot.at[rows], sems.at[1 + g]))
        get_pot[g].start()
    get_map.wait()

    dest, label = place[...] >> 10, (place[...] & (ROWS - 1)) + 1
    sub = iota((128, 128), 0)
    before = jnp.concatenate([one_hot(sub < iota((128, 128), 1)), one_hot(sub >= 0)], axis=1)
    hits = [dest[b : b + 1, :] == sub for b in range(8)]
    hot = [one_hot(h) for h in hits]
    counts = mm(jnp.concatenate(hot, axis=0), before)
    carry = jnp.zeros((128, 128), F32)
    ranks = []
    for b in range(8):
        part = counts[b * 128 : b * 128 + 128]
        ranks.append(jnp.sum(jnp.where(hits[b], part[:, :128] + carry, 0.0), axis=0, keepdims=True))
        carry = carry + part[:, 128:]
    low = sub & (CAP - 1)
    ranked = []
    for b in range(8):
        lanes = pl.ds(b * 128, 128)
        for r in range(HALF):
            weight = jnp.where(ranks[b] == r, 1.0, jnp.where(ranks[b] == r + HALF, 256.0, 0.0))
            block = times_row(hot[b], weight)
            for g in range(4):
                sel[pl.ds(g * 256 + r * 32, 32), lanes] = block[g * 32 : g * 32 + 32]
        ranked.append(one_hot(ranks[b].astype(I32) == low))

    for g in range(8):
        if g == 0:
            get_pot[0].wait()
            get_pot[1].wait()
        if g == 4:
            get_pot[2].wait()
            get_pot[3].wait()
            for k in range(4):
                for n in range(TILES):
                    cols = pl.ds(n * 256, 256)
                    half[pl.ds(k * 256, 256), cols] = mm(sel[pl.ds(k * 256, 256), 0:512], dig[0:512, cols])
        rows = pl.ds(g * 128, 128)
        x = pot[rows, :]
        top = jnp.max(jnp.abs(x), axis=1, keepdims=True)
        step = jnp.maximum(top * (1.0 / 32766.0), 2.0**-100)
        expo = jnp.floor(jnp.log2(step) + 1e-3)
        power = jnp.exp2(expo).astype(BF16).astype(F32)
        mant = jnp.maximum(jnp.ceil((step / power - 1.0) * 64.0), 0.0)
        scale = power * (1.0 + mant * (1.0 / 64.0))
        q = jnp.round(x * (1.0 / scale)) + 32768.0
        hi = jnp.floor(q * (1.0 / 256.0))
        lo = q - hi * 256.0
        for n in range(TILES):
            dig[rows, pl.ds(n * 256, 128)] = hi[:, n * 128 : n * 128 + 128].astype(BF16)
            dig[rows, pl.ds(n * 256 + 128, 128)] = lo[:, n * 128 : n * 128 + 128].astype(BF16)
        lane = iota((128, 128), 1)
        head[rows, :] = jnp.where(lane == 0, expo + 128.0, jnp.where(lane == 1, mant, 0.0)).astype(BF16)
    eye = one_hot(iota((16, 128), 0) == iota((16, 128), 1))
    codes = lax.dot_general(eye, head[...], NT, preferred_element_type=F32)

    digits = [[], [], [], []]
    for b in range(8):
        lab = label[b : b + 1, :]
        cols = slice(b * 128, b * 128 + 128)
        for k, row in enumerate(
            ((lab >> 7).astype(F32), (lab & 127).astype(F32), codes[0:1, cols], codes[1:2, cols])
        ):
            digits[k].append(times_row(hot[b], row))
    left = jnp.concatenate([jnp.concatenate(d, axis=1) for d in digits], axis=0)
    meta = lax.dot_general(left, jnp.concatenate(ranked, axis=1), NT, preferred_element_type=F32).astype(I32)
    words = jnp.where(
        iota((128, 128), 1) < CAP, meta[0:128] * 128 + meta[128:256], meta[256:384] * 128 + meta[384:512]
    )
    msg[pl.ds(LINES - 1, DEV, stride=LINES), :] = words

    put = []
    for g in range(4):
        for n in range(TILES):
            cols = pl.ds(n * 256, 256)
            both = half[pl.ds(g * 256, 256), cols] + mm(sel[pl.ds(g * 256, 256), 512:1024], dig[512:1024, cols])
            both = both.astype(I32)
            w = (both[:, :128] << 16) | both[:, 128:]
            for r in range(HALF):
                msg[pl.ds(g * 32 * LINES + n * HALF + r, 32, stride=LINES), :] = w[r * 32 : r * 32 + 32]
        lines = pl.ds(g * 32 * LINES, 32 * LINES)
        put.append(pltpu.make_async_copy(msg.at[lines], out_hbm.at[lines], sems.at[5 + g]))
        put[g].start()
    for copy in put:
        copy.wait()


def pack(leaf_to_panel, potentials):
    return pl.pallas_call(
        pack_kernel,
        out_shape=jax.ShapeDtypeStruct((DEV * LINES, 128), I32),
        in_specs=[HBM, HBM],
        out_specs=HBM,
        scratch_shapes=[
            pltpu.VMEM((8, 128), I32),
            pltpu.VMEM((ROWS, BW), F32),
            pltpu.VMEM((DEV * LINES, 128), I32),
            pltpu.VMEM((DEV * HALF, ROWS), BF16),
            pltpu.VMEM((ROWS, 2 * BW), BF16),
            pltpu.VMEM((ROWS, 128), BF16),
            pltpu.VMEM((ROWS, 2 * BW), F32),
            pltpu.SemaphoreType.DMA((9,)),
        ],
        compiler_params=pltpu.CompilerParams(vmem_limit_bytes=60 * 2**20),
        cost_estimate=pl.CostEstimate(flops=2 * DEV * CAP * ROWS * 2 * BW, bytes_accessed=4 * 2**20, transcendentals=0),
        name="pack_rows",
    )(leaf_to_panel.reshape(8, 128), potentials)


def place_kernel(msg_ref, out, sel, dig):
    heads = msg_ref[pl.ds(LINES - 1, DEV, stride=LINES), :]
    turned = jnp.transpose(heads.astype(F32)).astype(I32)
    target = turned[0:CAP] - 1
    high, low = target >> 7, target & 127
    sub = iota((128, 128), 0)
    lane = iota((128, 128), 1)
    for c in range(CAP):
        hot = one_hot(low[c : c + 1] == sub)
        for g in range(4):
            row = jnp.where(high[c : c + 1] == g, 1.0, jnp.where(high[c : c + 1] == g + 4, 256.0, 0.0))
            sel[pl.ds(g * 128, 128), pl.ds(c * 128, 128)] = times_row(hot, row)
        code = heads[:, CAP + c : CAP + c + 1]
        code = jnp.where(lane == 0, code >> 7, jnp.where(lane == 1, code & 127, 0))
        dig[pl.ds(c * 128, 128), pl.ds(2 * BW, 128)] = code.astype(F32).astype(BF16)
    for n in range(TILES):
        for r in range(HALF):
            w = msg_ref[pl.ds(n * HALF + r, DEV, stride=LINES), :]
            for c, hi, lo in ((r, (w >> 16) & 255, w & 255), (r + HALF, (w >> 24) & 255, (w >> 8) & 255)):
                dig[pl.ds(c * 128, 128), pl.ds(n * 256, 128)] = hi.astype(F32).astype(BF16)
                dig[pl.ds(c * 128, 128), pl.ds(n * 256 + 128, 128)] = lo.astype(F32).astype(BF16)
    for part in (sel[...],):
        codes = mm(part, dig[:, pl.ds(2 * BW, 128)])[:, 0:2].astype(I32)
        scales = []
        for code in (codes & 255, codes >> 8):
            power = jnp.exp2(code[:, 0:1].astype(F32) - 128.0).astype(BF16).astype(F32)
            scales.append(power * (1.0 + code[:, 1:2].astype(F32) * (1.0 / 64.0)))
        spots = [pl.ds(h * 512, 512) for h in range(2)]
        for n in range(TILES):
            cols = pl.ds(n * 128, 128)
            both = mm(part, dig[:, pl.ds(n * 256, 256)]).astype(I32)
            hi, lo = both[:, :128], both[:, 128:]
            values = (((hi & 255) << 8) | (lo & 255), (hi & 0xFF00) | (lo >> 8))
            for h in range(2):
                out[spots[h], cols] = (values[h] - 32768).astype(F32) * scales[h]


def place(arrived):
    return pl.pallas_call(
        place_kernel,
        out_shape=jax.ShapeDtypeStruct((ROWS, BW), F32),
        in_specs=[VMEM],
        out_specs=VMEM,
        scratch_shapes=[
            pltpu.VMEM((ROWS // 2, CAP * 128), BF16),
            pltpu.VMEM((CAP * 128, 2 * BW + 128), BF16),
        ],
        compiler_params=pltpu.CompilerParams(vmem_limit_bytes=40 * 2**20),
        cost_estimate=pl.CostEstimate(flops=DEV * CAP * ROWS * 2 * BW, bytes_accessed=4 * 2**20, transcendentals=0),
        name="place_rows",
    )(arrived)


def add_kernel(me_ref, placed_ref, own_ref, near_ref, far_ref, out_hbm, out, sems):
    lane = iota((1, 128), 1)
    own, adjacent, other = (ref[SLOTS : SLOTS + 1, 0:128] for ref in (own_ref, near_ref, far_ref))
    rows = jnp.where(lane < SLOTS, own, jnp.where(lane < 2 * SLOTS, adjacent, other)).astype(I32)
    target = jnp.where((rows < 0) | (lane >= 3 * SLOTS), -1, (rows - me_ref[0] * ROWS) & (TOTAL - 1))
    near = jnp.concatenate([own_ref[0:SLOTS], near_ref[0:SLOTS], far_ref[0:SLOTS], jnp.zeros((SLOTS, BW), F32)], axis=0)
    first = near.astype(BF16)
    near = jnp.concatenate([first, (near - first.astype(F32)).astype(BF16)], axis=0)
    sub = iota((256, 128), 0)
    put = []
    for g in range(4):
        hot = one_hot(target - g * 256 == sub)
        spot = pl.ds(g * 256, 256)
        out[spot, :] = placed_ref[spot, :] + mm(jnp.concatenate([hot, hot], axis=1), near)
        put.append(pltpu.make_async_copy(out.at[spot], out_hbm.at[spot], sems.at[g]))
        put[g].start()
    for copy in put:
        copy.wait()


def add_terms(me, placed, terms):
    return pl.pallas_call(
        add_kernel,
        out_shape=jax.ShapeDtypeStruct((ROWS, BW), F32),
        in_specs=[SMEM] + [VMEM] * 4,
        out_specs=HBM,
        scratch_shapes=[pltpu.VMEM((ROWS, BW), F32), pltpu.SemaphoreType.DMA((4,))],
        compiler_params=pltpu.CompilerParams(vmem_limit_bytes=12 * 2**20),
        cost_estimate=pl.CostEstimate(flops=2 * ROWS * 256 * BW, bytes_accessed=4 * 2**20, transcendentals=0),
        name="add_terms",
    )(me, placed, *terms)


def fetch_kernel(me_ref, own_cols, near_cols, far_cols, density_ref, msg_ref, own_ref, near_ref, far_ref, out_ref):
    base = me_ref[0] * ROWS
    cols = jnp.concatenate([own_cols[...], near_cols[...], far_cols[...], own_cols[...]], axis=1)
    at = ((cols - base) & (TOTAL - 1)).astype(F32)
    at = jnp.transpose(jnp.broadcast_to(at, (128, 128)))[0 : 3 * SLOTS].astype(I32)
    lane = iota((3 * SLOTS, 128), 1)
    hot = jnp.concatenate([one_hot(at - b * 128 == lane) for b in range(8)], axis=1)
    got = mm(hot, density_ref[...]).astype(BF16)
    own_ref[...] = got[0:SLOTS]
    near_ref[...] = got[SLOTS : 2 * SLOTS]
    far_ref[...] = got[2 * SLOTS :]


def fetch(me, cols, density, message):
    rows = jax.ShapeDtypeStruct((SLOTS, BW), BF16)
    return pl.pallas_call(
        fetch_kernel,
        out_shape=(rows, rows, rows, jax.ShapeDtypeStruct(message.shape, message.dtype)),
        in_specs=[SMEM] + [VMEM] * 4 + [HBM],
        out_specs=(VMEM, VMEM, VMEM, HBM),
        input_output_aliases={5: 3},
        compiler_params=pltpu.CompilerParams(vmem_limit_bytes=105 * 2**19),
        cost_estimate=pl.CostEstimate(flops=10**8, bytes_accessed=2**20, transcendentals=0),
        name="fetch_density",
    )(me, *(x.reshape(1, SLOTS) for x in cols), density, message)


STEP = 4


def term_kernel(count_ref, mats_ref, targets_ref, own_ref, far_ref, near_ref, out_ref, acc, vecs):
    step = pl.program_id(0)

    @pl.when(step == 0)
    def _():
        acc[...] = jnp.zeros_like(acc)
        got = own_ref[...].astype(F32) + near_ref[...].astype(F32) + far_ref[...].astype(F32)
        vecs[...] = jnp.concatenate([got, jnp.zeros((128 - SLOTS, BW), F32)], axis=0).astype(BF16)

    lane = iota((BW, 128), 1)
    total = acc[...]
    for k in range(STEP):
        prod = lax.dot_general(mats_ref[k], vecs[...], NT, preferred_element_type=F32)
        total = jnp.where(lane == step * STEP + k, prod, total)
    acc[...] = total

    @pl.when(step == SLOTS // STEP - 1)
    def _():
        live = iota((SLOTS, BW), 0) < count_ref[...]
        out_ref[0:SLOTS, :] = jnp.where(live, jnp.transpose(acc[...])[0:SLOTS], 0.0)
        slot = iota((1, 128), 1) & (SLOTS - 1)
        rows = jnp.concatenate([targets_ref[...]] * (128 // SLOTS), axis=1)
        rows = jnp.where(slot < count_ref[...], rows, -1).astype(F32)
        for n in range(TILES):
            out_ref[SLOTS : SLOTS + 8, n * 128 : n * 128 + 128] = jnp.broadcast_to(rows, (8, 128))


def make_terms(count, mats, targets, rows):
    def whole(rows, width):
        return pl.BlockSpec((rows, width), lambda i: (0, 0))

    return pl.pallas_call(
        term_kernel,
        grid=(SLOTS // STEP,),
        out_shape=jax.ShapeDtypeStruct((SLOTS + 8, BW), F32),
        in_specs=[whole(1, 1), pl.BlockSpec((STEP, BW, BW), lambda i: (i, 0, 0)), whole(1, SLOTS)] + [whole(SLOTS, BW)] * 3,
        out_specs=whole(SLOTS + 8, BW),
        scratch_shapes=[pltpu.VMEM((BW, 128), F32), pltpu.VMEM((128, BW), BF16)],
        compiler_params=pltpu.CompilerParams(vmem_limit_bytes=20 * 2**20),
        cost_estimate=pl.CostEstimate(flops=6 * 10**10, bytes_accessed=SLOTS * BW * BW * 2, transcendentals=0),
        name="near_terms",
    )(count, mats, targets, *rows)


def swap_near(value):
    return lax.ppermute(value, AXES, [(i, i ^ 1) for i in range(DEV)])


def swap_far(value):
    return lax.ppermute(value, AXES, [(i, (i - 1 + 2 * (i % 2)) % DEV) for i in range(DEV)])


def on_device(potentials, leaf_to_panel, density, corrections, correction_rows, correction_cols, block_count):
    me = lax.axis_index(AXES).astype(I32).reshape(1)
    cols = (correction_cols, swap_far(correction_cols), swap_near(correction_cols))
    message = pack(leaf_to_panel, potentials)
    own, for_far, for_near, message = fetch(me, cols, density, message)
    rows = (own, swap_far(for_far), swap_near(for_near))
    arrived = lax.all_to_all(
        message.reshape(DEV, LINES, 1, 128), AXES, split_axis=0, concat_axis=0, tiled=True
    ).reshape(DEV * LINES, 128)
    term = make_terms(block_count.reshape(1, 1), corrections, correction_rows.reshape(1, SLOTS), rows)
    terms = (term, swap_far(term), swap_near(term))
    return add_terms(me, place(arrived), terms)


def solution(mesh):
    rows = P(AXES, None)
    flat = P(AXES)
    return jax.shard_map(
        on_device,
        mesh=mesh,
        in_specs=(rows, flat, rows, P(AXES, None, None), flat, flat, flat),
        out_specs=rows,
        check_vma=False,
    )
```

```python
import functools

import jax
import jax.numpy as jnp
from jax import lax
from jax.experimental import pallas as pl
from jax.experimental.pallas import tpu as pltpu
from jax.sharding import PartitionSpec as P

AXES = ("leaf", "panel")
DEV = 128
CAP = 16
HALF = CAP // 2
ROWS = 1024
BW = 384
TILES = BW // 128
LINES = HALF * TILES + 1
SLOTS = 32
TOTAL = DEV * ROWS
F32, BF16, I32 = jnp.float32, jnp.bfloat16, jnp.int32
NT = (((1,), (1,)), ((), ()))
VMEM = pl.BlockSpec(memory_space=pltpu.VMEM)
SMEM = pl.BlockSpec(memory_space=pltpu.SMEM)
HBM = pl.BlockSpec(memory_space=pltpu.HBM)


def iota(shape, dim):
    return lax.broadcasted_iota(I32, shape, dim)


def one_hot(mask):
    return jnp.where(mask, 1.0, 0.0).astype(BF16)


def row16(row):
    return jnp.broadcast_to(row, (16, 128)).astype(BF16)[None]


def times_row(block, row):
    return (block.reshape(8, 16, 128) * row16(row)).reshape(128, 128)


def mm(a, b):
    return jnp.dot(a, b, preferred_element_type=F32)


def pack_kernel(place, pot_hbm, out_hbm, pot, msg, sel, dig, head, half, sems):
    get_pot = []
    for g in range(4):
        rows = pl.ds(g * 256, 256)
        get_pot.append(pltpu.make_async_copy(pot_hbm.at[rows], pot.at[rows], sems.at[1 + g]))
        get_pot[g].start()

    dest, label = place[...] >> 10, (place[...] & (ROWS - 1)) + 1
    sub = iota((128, 128), 0)
    before = jnp.concatenate([one_hot(sub < iota((128, 128), 1)), one_hot(sub >= 0)], axis=1)
    hits = [dest[b : b + 1, :] == sub for b in range(8)]
    hot = [one_hot(h) for h in hits]
    counts = mm(jnp.concatenate(hot, axis=0), before)
    carry = jnp.zeros((128, 128), F32)
    ranks = []
    for b in range(8):
        part = counts[b * 128 : b * 128 + 128]
        ranks.append(jnp.sum(jnp.where(hits[b], part[:, :128] + carry, 0.0), axis=0, keepdims=True))
        carry = carry + part[:, 128:]
    low = sub & (CAP - 1)
    ranked = []
    for b in range(8):
        lanes = pl.ds(b * 128, 128)
        for r in range(HALF):
            weight = jnp.where(ranks[b] == r, 1.0, jnp.where(ranks[b] == r + HALF, 256.0, 0.0))
            block = times_row(hot[b], weight)
            for g in range(4):
                sel[pl.ds(g * 256 + r * 32, 32), lanes] = block[g * 32 : g * 32 + 32]
        ranked.append(one_hot(ranks[b].astype(I32) == low))

    for g in range(8):
        if g == 0:
            get_pot[0].wait()
            get_pot[1].wait()
        if g == 4:
            get_pot[2].wait()
            get_pot[3].wait()
            for k in range(4):
                for n in range(TILES):
                    cols = pl.ds(n * 256, 256)
                    half[pl.ds(k * 256, 256), cols] = mm(sel[pl.ds(k * 256, 256), 0:512], dig[0:512, cols])
        rows = pl.ds(g * 128, 128)
        x = pot[rows, :]
        top = jnp.max(jnp.abs(x), axis=1, keepdims=True)
        step = jnp.maximum(top * (1.0 / 32766.0), 2.0**-100)
        expo = jnp.floor(jnp.log2(step) + 1e-3)
        power = jnp.exp2(expo).astype(BF16).astype(F32)
        mant = jnp.maximum(jnp.ceil((step / power - 1.0) * 64.0), 0.0)
        scale = power * (1.0 + mant * (1.0 / 64.0))
        q = jnp.round(x * (1.0 / scale)) + 32768.0
        hi = jnp.floor(q * (1.0 / 256.0))
        lo = q - hi * 256.0
        for n in range(TILES):
            dig[rows, pl.ds(n * 256, 128)] = hi[:, n * 128 : n * 128 + 128].astype(BF16)
            dig[rows, pl.ds(n * 256 + 128, 128)] = lo[:, n * 128 : n * 128 + 128].astype(BF16)
        lane = iota((128, 128), 1)
        head[rows, :] = jnp.where(lane == 0, expo + 128.0, jnp.where(lane == 1, mant, 0.0)).astype(BF16)
    eye = one_hot(iota((16, 128), 0) == iota((16, 128), 1))
    codes = lax.dot_general(eye, head[...], NT, preferred_element_type=F32)

    digits = [[], [], [], []]
    for b in range(8):
        lab = label[b : b + 1, :]
        cols = slice(b * 128, b * 128 + 128)
        for k, row in enumerate(
            ((lab >> 7).astype(F32), (lab & 127).astype(F32), codes[0:1, cols], codes[1:2, cols])
        ):
            digits[k].append(times_row(hot[b], row))
    left = jnp.concatenate([jnp.concatenate(d, axis=1) for d in digits], axis=0)
    meta = lax.dot_general(left, jnp.concatenate(ranked, axis=1), NT, preferred_element_type=F32).astype(I32)
    words = jnp.where(
        iota((128, 128), 1) < CAP, meta[0:128] * 128 + meta[128:256], meta[256:384] * 128 + meta[384:512]
    )
    msg[pl.ds(LINES - 1, DEV, stride=LINES), :] = words

    put = []
    for g in range(4):
        for n in range(TILES):
            cols = pl.ds(n * 256, 256)
            both = half[pl.ds(g * 256, 256), cols] + mm(sel[pl.ds(g * 256, 256), 512:1024], dig[512:1024, cols])
            both = both.astype(I32)
            w = (both[:, :128] << 16) | both[:, 128:]
            for r in range(HALF):
                msg[pl.ds(g * 32 * LINES + n * HALF + r, 32, stride=LINES), :] = w[r * 32 : r * 32 + 32]
        lines = pl.ds(g * 32 * LINES, 32 * LINES)
        put.append(pltpu.make_async_copy(msg.at[lines], out_hbm.at[lines], sems.at[5 + g]))
        put[g].start()
    for copy in put:
        copy.wait()


def pack(leaf_to_panel, potentials):
    return pl.pallas_call(
        pack_kernel,
        out_shape=jax.ShapeDtypeStruct((DEV * LINES, 128), I32),
        in_specs=[VMEM, HBM],
        out_specs=HBM,
        scratch_shapes=[
            pltpu.VMEM((ROWS, BW), F32),
            pltpu.VMEM((DEV * LINES, 128), I32),
            pltpu.VMEM((DEV * HALF, ROWS), BF16),
            pltpu.VMEM((ROWS, 2 * BW), BF16),
            pltpu.VMEM((ROWS, 128), BF16),
            pltpu.VMEM((ROWS, 2 * BW), F32),
            pltpu.SemaphoreType.DMA((9,)),
        ],
        compiler_params=pltpu.CompilerParams(vmem_limit_bytes=105 * 2**19),
        cost_estimate=pl.CostEstimate(flops=2 * DEV * CAP * ROWS * 2 * BW, bytes_accessed=4 * 2**20, transcendentals=0),
        name="pack_rows",
    )(leaf_to_panel.reshape(8, 128), potentials)


def place_kernel(msg_ref, out, sel, dig):
    heads = msg_ref[pl.ds(LINES - 1, DEV, stride=LINES), :]
    turned = jnp.transpose(heads.astype(F32)).astype(I32)
    target = turned[0:CAP] - 1
    high, low = target >> 7, target & 127
    sub = iota((128, 128), 0)
    lane = iota((128, 128), 1)
    for c in range(CAP):
        hot = one_hot(low[c : c + 1] == sub)
        for g in range(4):
            row = jnp.where(high[c : c + 1] == g, 1.0, jnp.where(high[c : c + 1] == g + 4, 256.0, 0.0))
            sel[pl.ds(g * 128, 128), pl.ds(c * 128, 128)] = times_row(hot, row)
        code = heads[:, CAP + c : CAP + c + 1]
        code = jnp.where(lane == 0, code >> 7, jnp.where(lane == 1, code & 127, 0))
        dig[pl.ds(c * 128, 128), pl.ds(2 * BW, 128)] = code.astype(F32).astype(BF16)
    for n in range(TILES):
        for r in range(HALF):
            w = msg_ref[pl.ds(n * HALF + r, DEV, stride=LINES), :]
            for c, hi, lo in ((r, (w >> 16) & 255, w & 255), (r + HALF, (w >> 24) & 255, (w >> 8) & 255)):
                dig[pl.ds(c * 128, 128), pl.ds(n * 256, 128)] = hi.astype(F32).astype(BF16)
                dig[pl.ds(c * 128, 128), pl.ds(n * 256 + 128, 128)] = lo.astype(F32).astype(BF16)
    for part in (sel[...],):
        codes = mm(part, dig[:, pl.ds(2 * BW, 128)])[:, 0:2].astype(I32)
        scales = []
        for code in (codes & 255, codes >> 8):
            power = jnp.exp2(code[:, 0:1].astype(F32) - 128.0).astype(BF16).astype(F32)
            scales.append(power * (1.0 + code[:, 1:2].astype(F32) * (1.0 / 64.0)))
        spots = [pl.ds(h * 512, 512) for h in range(2)]
        for n in range(TILES):
            cols = pl.ds(n * 128, 128)
            both = mm(part, dig[:, pl.ds(n * 256, 256)]).astype(I32)
            hi, lo = both[:, :128], both[:, 128:]
            values = (((hi & 255) << 8) | (lo & 255), (hi & 0xFF00) | (lo >> 8))
            for h in range(2):
                out[spots[h], cols] = (values[h] - 32768).astype(F32) * scales[h]


def place(arrived):
    return pl.pallas_call(
        place_kernel,
        out_shape=jax.ShapeDtypeStruct((ROWS, BW), F32),
        in_specs=[VMEM],
        out_specs=VMEM,
        scratch_shapes=[
            pltpu.VMEM((ROWS // 2, CAP * 128), BF16),
            pltpu.VMEM((CAP * 128, 2 * BW + 128), BF16),
        ],
        compiler_params=pltpu.CompilerParams(vmem_limit_bytes=40 * 2**20),
        cost_estimate=pl.CostEstimate(flops=DEV * CAP * ROWS * 2 * BW, bytes_accessed=4 * 2**20, transcendentals=0),
        name="place_rows",
    )(arrived)


def add_kernel(me_ref, placed_ref, own_ref, near_ref, far_ref, out_hbm, out, sems):
    lane = iota((1, 128), 1)
    own, adjacent, other = (ref[SLOTS : SLOTS + 1, 0:128] for ref in (own_ref, near_ref, far_ref))
    rows = jnp.where(lane < SLOTS, own, jnp.where(lane < 2 * SLOTS, adjacent, other)).astype(I32)
    target = jnp.where((rows < 0) | (lane >= 3 * SLOTS), -1, (rows - me_ref[0] * ROWS) & (TOTAL - 1))
    near = jnp.concatenate([own_ref[0:SLOTS], near_ref[0:SLOTS], far_ref[0:SLOTS], jnp.zeros((SLOTS, BW), F32)], axis=0)
    first = near.astype(BF16)
    near = jnp.concatenate([first, (near - first.astype(F32)).astype(BF16)], axis=0)
    sub = iota((256, 128), 0)
    put = []
    for g in range(4):
        hot = one_hot(target - g * 256 == sub)
        spot = pl.ds(g * 256, 256)
        out[spot, :] = placed_ref[spot, :] + mm(jnp.concatenate([hot, hot], axis=1), near)
        put.append(pltpu.make_async_copy(out.at[spot], out_hbm.at[spot], sems.at[g]))
        put[g].start()
    for copy in put:
        copy.wait()


def add_terms(me, placed, terms):
    return pl.pallas_call(
        add_kernel,
        out_shape=jax.ShapeDtypeStruct((ROWS, BW), F32),
        in_specs=[SMEM] + [VMEM] * 4,
        out_specs=HBM,
        scratch_shapes=[pltpu.VMEM((ROWS, BW), F32), pltpu.SemaphoreType.DMA((4,))],
        compiler_params=pltpu.CompilerParams(vmem_limit_bytes=12 * 2**20),
        cost_estimate=pl.CostEstimate(flops=2 * ROWS * 256 * BW, bytes_accessed=4 * 2**20, transcendentals=0),
        name="add_terms",
    )(me, placed, *terms)


def fetch_kernel(me_ref, own_cols, near_cols, far_cols, density_ref, msg_ref, own_ref, near_ref, far_ref, out_ref):
    base = me_ref[0] * ROWS
    cols = jnp.concatenate([own_cols[...], near_cols[...], far_cols[...], own_cols[...]], axis=1)
    at = ((cols - base) & (TOTAL - 1)).astype(F32)
    at = jnp.transpose(jnp.broadcast_to(at, (128, 128)))[0 : 3 * SLOTS].astype(I32)
    lane = iota((3 * SLOTS, 128), 1)
    hot = jnp.concatenate([one_hot(at - b * 128 == lane) for b in range(8)], axis=1)
    got = mm(hot, density_ref[...]).astype(BF16)
    own_ref[...] = got[0:SLOTS]
    near_ref[...] = got[SLOTS : 2 * SLOTS]
    far_ref[...] = got[2 * SLOTS :]


def fetch(me, cols, density, message):
    rows = jax.ShapeDtypeStruct((SLOTS, BW), BF16)
    return pl.pallas_call(
        fetch_kernel,
        out_shape=(rows, rows, rows, jax.ShapeDtypeStruct(message.shape, message.dtype)),
        in_specs=[SMEM] + [VMEM] * 4 + [HBM],
        out_specs=(VMEM, VMEM, VMEM, HBM),
        input_output_aliases={5: 3},
        compiler_params=pltpu.CompilerParams(vmem_limit_bytes=105 * 2**19),
        cost_estimate=pl.CostEstimate(flops=10**8, bytes_accessed=2**20, transcendentals=0),
        name="fetch_density",
    )(me, *(x.reshape(1, SLOTS) for x in cols), density, message)


STEP = 4


def term_kernel(count_ref, mats_ref, targets_ref, own_ref, far_ref, near_ref, out_ref, acc, vecs):
    step = pl.program_id(0)

    @pl.when(step == 0)
    def _():
        acc[...] = jnp.zeros_like(acc)
        got = own_ref[...].astype(F32) + near_ref[...].astype(F32) + far_ref[...].astype(F32)
        vecs[...] = jnp.concatenate([got, jnp.zeros((128 - SLOTS, BW), F32)], axis=0).astype(BF16)

    lane = iota((BW, 128), 1)
    total = acc[...]
    for k in range(STEP):
        prod = lax.dot_general(mats_ref[k], vecs[...], NT, preferred_element_type=F32)
        total = jnp.where(lane == step * STEP + k, prod, total)
    acc[...] = total

    @pl.when(step == SLOTS // STEP - 1)
    def _():
        live = iota((SLOTS, BW), 0) < count_ref[...]
        out_ref[0:SLOTS, :] = jnp.where(live, jnp.transpose(acc[...])[0:SLOTS], 0.0)
        slot = iota((1, 128), 1) & (SLOTS - 1)
        rows = jnp.concatenate([targets_ref[...]] * (128 // SLOTS), axis=1)
        rows = jnp.where(slot < count_ref[...], rows, -1).astype(F32)
        for n in range(TILES):
            out_ref[SLOTS : SLOTS + 8, n * 128 : n * 128 + 128] = jnp.broadcast_to(rows, (8, 128))


def make_terms(count, mats, targets, rows):
    def whole(rows, width):
        return pl.BlockSpec((rows, width), lambda i: (0, 0))

    return pl.pallas_call(
        term_kernel,
        grid=(SLOTS // STEP,),
        out_shape=jax.ShapeDtypeStruct((SLOTS + 8, BW), F32),
        in_specs=[whole(1, 1), pl.BlockSpec((STEP, BW, BW), lambda i: (i, 0, 0)), whole(1, SLOTS)] + [whole(SLOTS, BW)] * 3,
        out_specs=whole(SLOTS + 8, BW),
        scratch_shapes=[pltpu.VMEM((BW, 128), F32), pltpu.VMEM((128, BW), BF16)],
        compiler_params=pltpu.CompilerParams(vmem_limit_bytes=20 * 2**20),
        cost_estimate=pl.CostEstimate(flops=6 * 10**10, bytes_accessed=SLOTS * BW * BW * 2, transcendentals=0),
        name="near_terms",
    )(count, mats, targets, *rows)


def swap_near(value):
    return lax.ppermute(value, AXES, [(i, i ^ 1) for i in range(DEV)])


def swap_far(value):
    return lax.ppermute(value, AXES, [(i, (i - 1 + 2 * (i % 2)) % DEV) for i in range(DEV)])


def on_device(potentials, leaf_to_panel, density, corrections, correction_rows, correction_cols, block_count):
    me = lax.axis_index(AXES).astype(I32).reshape(1)
    cols = (correction_cols, swap_far(correction_cols), swap_near(correction_cols))
    message = pack(leaf_to_panel, potentials)
    own, for_far, for_near, message = fetch(me, cols, density, message)
    rows = (own, swap_far(for_far), swap_near(for_near))
    arrived = lax.all_to_all(
        message.reshape(DEV, LINES, 1, 128), AXES, split_axis=0, concat_axis=0, tiled=True
    ).reshape(DEV * LINES, 128)
    term = make_terms(block_count.reshape(1, 1), corrections, correction_rows.reshape(1, SLOTS), rows)
    terms = (term, swap_far(term), swap_near(term))
    return add_terms(me, place(arrived), terms)


def solution(mesh):
    rows = P(AXES, None)
    flat = P(AXES)
    return jax.shard_map(
        on_device,
        mesh=mesh,
        in_specs=(rows, flat, rows, P(AXES, None, None), flat, flat, flat),
        out_specs=rows,
        check_vma=False,
    )
```
